256 devices in a mesh: batch: 16 (over y_lo, z), tensor: 16 (over x, y_hi, core).
Axes of the slice: x: 4, y: 4 (y_hi: 2, y_lo: 2; y = y_hi * 2 + y_lo), z: 8, core: 2. Of those that a mesh axis runs over, the one named last changes fastest.
Arguments:
- teacher_hidden: bfloat16 [16384, 10240], P('batch', 'tensor')
- teacher_down: bfloat16 [10240, 5120], P('tensor')
- teacher_bias: float32 [5120], P('tensor')
- teacher_resid: bfloat16 [16384, 5120], P('batch', 'tensor')
- student_feat: bfloat16 [16384, 1792], P('batch', 'tensor')
- norm_gain: float32 [1792], replicated, may hold values from 0.25 to 1.75
- norm_shift: float32 [1792], replicated, may hold values from -3 to 3
- head_weight: bfloat16 [1792, 5120], P(None, 'tensor')
- head_bias: float32 [5120], P('tensor')
- mask_index: int32 [16, 416], P('batch'), may hold values from 0 to 1023, as said below
Outputs:
- loss: float32 [], replicated
- grad_student: bfloat16 [16384, 1792], P('batch', 'tensor')
- grad_head_weight: float32 [1792, 5120], P(None, 'tensor')
- grad_head_bias: float32 [5120], P('tensor')
- grad_gain: float32 [1792], P('tensor')
- grad_shift: float32 [1792], P('tensor')
The draws below stay inside these ranges and needn't reach their ends.
Inputs may be any that keep to these rules, and one draw needn't show every extreme that they name: `mask_index`: each row lists 416 distinct patch indices of its image, in no particular order.
All inputs are finite; a program needn't handle non-finite values.
Results may differ from the reference program's by a relative error of at most 0.024.
Values may be sent and summed in bfloat16 or wider, within the bound.
No kernel may reach another device: no remote copies, remote signals or barrier semaphores. Data moves between devices by JAX's collectives and lax.ppermute only.
A program may use at most 128 MiB of HBM per device.

```python
import math
import jax
import jax.numpy as jnp
from jax import lax

DT = 5120
FT = 10240
DS = 1792
P_SIZE = 1024
MASKED = 416
LOSS_SCALE = 1024
IMAGES = 16
N_TENSOR = 16


def spread_scale(key, length, lowest, highest):
    return jnp.exp(jax.random.uniform(key, (length,), jnp.float32, math.log(lowest), math.log(highest)))


def column_ramp(key, width):
    return 3.0 ** (jnp.arange(width, dtype=jnp.float32) / width) * spread_scale(key, width, 1.0, 2.0)


def shared_columns(key):
    return jax.random.normal(key, (DT,), jnp.float32)


def draw_teacher_hidden(key, part):
    key = jax.random.fold_in(key, 1)
    first_key, second_key = jax.random.split(key)
    values = jax.random.normal(first_key, (IMAGES * P_SIZE, FT), jnp.float32)
    scales = spread_scale(second_key, IMAGES * P_SIZE, 1.0, 4.0)
    return (jax.nn.gelu(values * 1.5) * scales[:, None]).astype(jnp.bfloat16)


def draw_teacher_down(key, part):
    key = jax.random.fold_in(key, 2)
    first_key, second_key = jax.random.split(key)
    values = jax.random.normal(first_key, (FT, DT), jnp.float32)
    return (values * FT ** (-0.5) * column_ramp(second_key, DT)[None, :]).astype(jnp.bfloat16)


def draw_teacher_bias(key, part):
    common = shared_columns(key)
    key = jax.random.fold_in(key, 7)
    own = 0.5 * jax.random.normal(key, (DT,), jnp.float32)
    return 4.0 * common + own


def draw_teacher_resid(key, part):
    key = jax.random.fold_in(key, 3)
    first_key, second_key, third_key = jax.random.split(key, 3)
    values = jax.random.normal(first_key, (IMAGES * P_SIZE, DT), jnp.float32)
    scales = spread_scale(second_key, IMAGES * P_SIZE, 1.0, 4.0)
    return (values * scales[:, None] * column_ramp(third_key, DT)[None, :]).astype(jnp.bfloat16)


def draw_student_feat(key, part):
    key = jax.random.fold_in(key, 4)
    first_key, second_key, third_key, fourth_key = jax.random.split(key, 4)
    values = jax.random.normal(first_key, (IMAGES * P_SIZE, DS), jnp.float32)
    scales = spread_scale(second_key, IMAGES * P_SIZE, 1.0, 4.0)
    offsets = jax.random.normal(fourth_key, (IMAGES * P_SIZE,), jnp.float32)
    return ((values * column_ramp(third_key, DS)[None, :] + offsets[:, None]) * scales[:, None]).astype(jnp.bfloat16)


def draw_head_weight(key, part):
    key = jax.random.fold_in(key, 5)
    first_key, second_key = jax.random.split(key)
    values = jax.random.normal(first_key, (DS, DT), jnp.float32)
    return (values * DS ** (-0.5) * column_ramp(second_key, DT)[None, :]).astype(jnp.bfloat16)


def draw_head_bias(key, part):
    common = shared_columns(key)
    key = jax.random.fold_in(key, 8)
    first_key, second_key = jax.random.split(key)
    own = 0.5 * jax.random.normal(first_key, (DT,), jnp.float32)
    factor = spread_scale(second_key, DT, 0.7, 1.4)
    return 4.0 * common * factor + own


def draw_mask_index(key, part):
    key = jax.random.fold_in(key, 6)
    image_keys = jax.random.split(key, IMAGES)

    def one_image(image_key):
        return jax.random.permutation(image_key, P_SIZE)[:MASKED]
    return jax.vmap(one_image)(image_keys).astype(jnp.int32)


def noise(rng, extent, deviation, limit, kind=jnp.bfloat16):
    array = jax.random.normal(rng, extent, jnp.float32) * deviation
    return jnp.minimum(jnp.maximum(array, -limit), limit).astype(kind)


def setup_inputs(seed: int = 0) -> dict:
    seeds = jax.random.split(jax.random.key(seed), 11)
    return {
        "teacher_hidden": draw_teacher_hidden(jax.random.fold_in(seeds[10], 71), 0),
        "teacher_down": draw_teacher_down(jax.random.fold_in(seeds[10], 71), 0),
        "teacher_bias": draw_teacher_bias(jax.random.fold_in(seeds[10], 71), 0),
        "teacher_resid": draw_teacher_resid(jax.random.fold_in(seeds[10], 71), 0),
        "student_feat": draw_student_feat(jax.random.fold_in(seeds[10], 71), 0),
        "norm_gain": jnp.clip(1.0 + 0.15 * jax.random.normal(seeds[5], (DS,), jnp.float32), 0.25, 1.75),
        "norm_shift": noise(seeds[6], (DS,), 0.5, 3.0, jnp.float32),
        "head_weight": draw_head_weight(jax.random.fold_in(seeds[10], 71), 0),
        "head_bias": draw_head_bias(jax.random.fold_in(seeds[10], 71), 0),
        "mask_index": draw_mask_index(jax.random.fold_in(seeds[10], 71), 0),
    }


epsilon = 1e-06

def reference(teacher_hidden, teacher_down, teacher_bias, teacher_resid, student_feat, norm_gain, norm_shift, head_weight, head_bias, mask_index):
    offsets = (jnp.arange(IMAGES, dtype=jnp.int32) * P_SIZE)[:, None]
    row_index = (mask_index.astype(jnp.int32) + offsets).reshape(-1)
    picked = teacher_hidden[row_index].astype(jnp.float32)
    width_part = FT // N_TENSOR
    blocks = picked.reshape(picked.shape[0], N_TENSOR, width_part).transpose(1, 0, 2)
    down_blocks = teacher_down.astype(jnp.float32).reshape(N_TENSOR, width_part, DT)

    def add_block(running, operands):
        product = jnp.dot(operands[0], operands[1], precision=lax.Precision.HIGHEST)
        rounded = lax.optimization_barrier(product.astype(jnp.bfloat16))
        return (running + rounded.astype(jnp.float32), None)
    initial = jnp.zeros((picked.shape[0], DT), jnp.float32)
    summed, _ = lax.scan(add_block, initial, (blocks, down_blocks))
    target = summed + teacher_resid[row_index].astype(jnp.float32) + teacher_bias[None, :]
    features = student_feat[row_index].astype(jnp.float32)
    row_mean = lax.optimization_barrier(jnp.mean(features, axis=1))
    variance = lax.optimization_barrier(jnp.mean(features * features, axis=1)) - row_mean * row_mean
    inv_std = lax.rsqrt(variance + epsilon)
    normed = (features - row_mean[:, None]) * inv_std[:, None]
    scaled = (normed * norm_gain + norm_shift).astype(jnp.bfloat16)
    predicted = jnp.dot(scaled, head_weight, preferred_element_type=jnp.float32) + head_bias[None, :]
    cross_sum = lax.optimization_barrier(jnp.sum(predicted * target, axis=1))
    pred_sq = lax.optimization_barrier(jnp.sum(predicted * predicted, axis=1))
    targ_sq = lax.optimization_barrier(jnp.sum(target * target, axis=1))
    pred_inv = lax.rsqrt(pred_sq + epsilon)
    targ_inv = lax.rsqrt(targ_sq + epsilon)
    cosine = cross_sum * pred_inv * targ_inv
    loss = jnp.sum(1.0 - cosine) / (IMAGES * MASKED)
    pred_grad = (-LOSS_SCALE * (target * (pred_inv * targ_inv)[:, None] - (cosine * pred_inv * pred_inv)[:, None] * predicted)).astype(jnp.bfloat16)
    grad_head_weight = jnp.dot(scaled.T, pred_grad, preferred_element_type=jnp.float32)
    grad_head_bias = lax.optimization_barrier(jnp.sum(pred_grad.astype(jnp.float32), axis=0))
    dscaled = jnp.dot(pred_grad, head_weight.T, preferred_element_type=jnp.float32)
    grad_gain = lax.optimization_barrier(jnp.sum(dscaled * normed, axis=0))
    grad_shift = lax.optimization_barrier(jnp.sum(dscaled, axis=0))
    dnormed = dscaled * norm_gain
    feat_grad = inv_std[:, None] * (dnormed - lax.optimization_barrier(jnp.mean(dnormed, axis=1, keepdims=True)) - normed * lax.optimization_barrier(jnp.mean(dnormed * normed, axis=1, keepdims=True)))
    grad_student = jnp.zeros((IMAGES * P_SIZE, DS), jnp.float32).at[row_index].set(feat_grad).astype(jnp.bfloat16)
    return (loss, grad_student, grad_head_weight, grad_head_bias, grad_gain, grad_shift)
```

```python
import functools

import jax
import jax.numpy as jnp
from jax import lax
from jax.experimental import pallas as pl
from jax.experimental.pallas import tpu as pltpu
from jax.sharding import PartitionSpec as P

LOSS_SCALE = 1024
epsilon = 1e-06
X, YH = 4, 2
YL, Z = 2, 8
CHIPS = X * YH
OFFSETS = [(dx, dy) for dx in range(X) for dy in range(YH)]
bf16, f32 = jnp.bfloat16, jnp.float32


def core_pairs():
    return [(t, t ^ 1) for t in range(2 * CHIPS)]


def chip_pairs(dx, dy):
    out = []
    for t in range(2 * CHIPS):
        x, y, c = t >> 2, (t >> 1) & 1, t & 1
        out.append((t, (((x + dx) % X) << 2) | ((y ^ dy) << 1) | c))
    return out


def batch_pairs(dy, dz):
    out = []
    for b in range(YL * Z):
        y, z = b // Z, b % Z
        out.append((b, (y ^ dy) * Z + (z + dz) % Z))
    return out


def to_core(x):
    return lax.ppermute(x, "tensor", core_pairs())


def to_chip(x, dx, dy):
    return lax.ppermute(x, "tensor", chip_pairs(dx, dy))


def to_batch(x, dy, dz):
    return lax.ppermute(x, "batch", batch_pairs(dy, dz))


def dot(a, b, dims):
    return lax.dot_general(a, b, (dims, ((), ())), preferred_element_type=f32)


def pick_kernel(mask_ref, hidden_ref, resid_ref, feat_ref, h_ref, r_ref, f_ref):
    rows = mask_ref.shape[1]
    patches = hidden_ref.shape[0]
    place = lax.broadcasted_iota(jnp.int32, (patches, rows), 0)
    one_hot = (place == mask_ref[...]).astype(f32).astype(bf16)
    for src, dst in ((feat_ref, f_ref), (resid_ref, r_ref), (hidden_ref, h_ref)):
        dst[...] = dot(one_hot, src[...], ((0,), (0,))).astype(bf16)


def pick(mask, hidden, resid, feat):
    rows = mask.shape[1]
    return pl.pallas_call(
        pick_kernel,
        out_shape=[jax.ShapeDtypeStruct((rows, a.shape[1]), bf16) for a in (hidden, resid, feat)],
        compiler_params=pltpu.CompilerParams(vmem_limit_bytes=40 << 20),
    )(mask, hidden, resid, feat)


def project_kernel(order_ref, h_ref, d_ref, out_ref):
    out_ref[...] = dot(h_ref[...], d_ref[...], ((1,), (0,))).astype(bf16)


def project(order, h, down):
    rows, depth = h.shape
    width = down.shape[1] // CHIPS
    return pl.pallas_call(
        project_kernel,
        grid_spec=pltpu.PrefetchScalarGridSpec(
            num_scalar_prefetch=1,
            grid=(CHIPS,),
            in_specs=[
                pl.BlockSpec((rows, depth), lambda i, s: (0, 0)),
                pl.BlockSpec((depth, width), lambda i, s: (0, s[i])),
            ],
            out_specs=pl.BlockSpec((None, rows, width), lambda i, s: (i, 0, 0)),
        ),
        out_shape=jax.ShapeDtypeStruct((CHIPS, rows, width), bf16),
        compiler_params=pltpu.CompilerParams(vmem_limit_bytes=40 << 20),
    )(order, h, down)


def project_add_kernel(order_ref, h_ref, d_ref, add_ref, *out_refs):
    i = pl.program_id(0)
    value = dot(h_ref[...], d_ref[...], ((1,), (0,))) + add_ref[...].astype(f32)
    for k, out in enumerate(out_refs):

        @pl.when(i == k)
        def _(out=out):
            out[...] = value.astype(out.dtype)


def project_add(order, h, down, add):
    rows, depth = h.shape
    width = down.shape[1] // CHIPS
    return pl.pallas_call(
        project_add_kernel,
        grid_spec=pltpu.PrefetchScalarGridSpec(
            num_scalar_prefetch=1,
            grid=(CHIPS,),
            in_specs=[
                pl.BlockSpec((rows, depth), lambda i, s: (0, 0)),
                pl.BlockSpec((depth, width), lambda i, s: (0, s[i])),
                pl.BlockSpec((None, rows, width), lambda i, s: (i, 0, 0)),
            ],
            out_specs=[pl.BlockSpec((rows, width), lambda i, s: (0, 0))] * CHIPS,
        ),
        out_shape=[jax.ShapeDtypeStruct((rows, width), f32 if k == 0 else bf16) for k in range(CHIPS)],
        compiler_params=pltpu.CompilerParams(vmem_limit_bytes=40 << 20),
    )(order, h, down, add)


def back_kernel(order_ref, pg_ref, w_ref, *out_refs):
    i = pl.program_id(0)
    value = dot(pg_ref[...], w_ref[...], ((1,), (1,)))
    for k, out in enumerate(out_refs):

        @pl.when(i == k)
        def _(out=out):
            out[...] = value.astype(out.dtype)


def back(order, pg, weight):
    rows, depth = pg.shape
    width = weight.shape[0] // CHIPS
    return pl.pallas_call(
        back_kernel,
        grid_spec=pltpu.PrefetchScalarGridSpec(
            num_scalar_prefetch=1,
            grid=(CHIPS,),
            in_specs=[
                pl.BlockSpec((rows, depth), lambda i, s: (0, 0)),
                pl.BlockSpec((width, depth), lambda i, s: (s[i], 0)),
            ],
            out_specs=[pl.BlockSpec((rows, width), lambda i, s: (0, 0))] * CHIPS,
        ),
        out_shape=[jax.ShapeDtypeStruct((rows, width), f32 if k == 0 else bf16) for k in range(CHIPS)],
        compiler_params=pltpu.CompilerParams(vmem_limit_bytes=40 << 20),
    )(order, pg, weight)


def on_device(
    teacher_hidden,
    teacher_down,
    teacher_bias,
    teacher_resid,
    student_feat,
    norm_gain,
    norm_shift,
    head_weight,
    head_bias,
    mask_index,
):
    masked = mask_index.shape[1]
    half = masked // 2
    patches = teacher_hidden.shape[0]
    feat_own = student_feat.shape[1]
    cols_own = head_weight.shape[1]
    full_width = head_weight.shape[0]
    feat_chip = 2 * feat_own
    t = lax.axis_index("tensor")
    b = lax.axis_index("batch")
    core, yh, x = t & 1, (t >> 1) & 1, t >> 2
    chip = t >> 1
    yl, z = b // Z, b % Z
    first = core == 0
    order = jnp.stack([((x + dx) % X) * YH + (yh ^ dy) for dx, dy in OFFSETS]).astype(jnp.int32)

    def both(mine, other, axis):
        return jnp.where(
            first, jnp.concatenate([mine, other], axis), jnp.concatenate([other, mine], axis)
        )

    def own_cols(a, width, of=None):
        return lax.dynamic_slice_in_dim(a, (core if of is None else of) * width, width, 1)

    mask = jnp.where(first, mask_index, jnp.roll(mask_index, half, 1))
    h_all, r_all, f_all = pick(mask, teacher_hidden, teacher_resid, student_feat)
    f_in = to_core(f_all[half:])
    part_other = project(order, h_all[half:], teacher_down)
    part_in = to_core(part_other)
    w_in = to_core(head_weight)
    r_in = to_core(r_all[half:])
    bias_in = to_core(jnp.stack([teacher_bias, head_bias]))

    f_chip = both(f_all[:half], f_in, 1)
    f_y = to_chip(f_chip, 0, 1)
    f_pair = jnp.where(yh == 0, jnp.stack([f_chip, f_y]), jnp.stack([f_y, f_chip]))
    f_blocks = jnp.stack([f_pair] + [to_chip(f_pair, dx, 0) for dx in range(1, X)])
    f_blocks = jnp.take(f_blocks, (x - jnp.arange(X)) % X, axis=0)
    feats = f_blocks.reshape(CHIPS, half, feat_chip).transpose(1, 0, 2).reshape(half, full_width)

    sums = project_add(order, h_all[:half], teacher_down, part_in)
    arrived = [to_chip(s, dx, dy) for s, (dx, dy) in zip(sums[1:], OFFSETS[1:], strict=True)]

    feat_float = feats.astype(f32)
    row_mean = jnp.mean(feat_float, axis=1)
    variance = jnp.mean(feat_float * feat_float, axis=1) - row_mean * row_mean
    inv_std = lax.rsqrt(variance + epsilon)
    normed = (feat_float - row_mean[:, None]) * inv_std[:, None]
    scaled = (normed * norm_gain + norm_shift).astype(bf16)
    weight = both(head_weight, w_in, 1)
    biases = both(jnp.stack([teacher_bias, head_bias]), bias_in, 1)
    predicted = dot(scaled, weight, ((1,), (0,))) + biases[1]
    weight_float = weight.astype(f32)
    gain_cols = jnp.sum(weight_float * norm_gain[:, None], axis=0)
    shift_cols = jnp.sum(weight_float * norm_shift[:, None], axis=0) + biases[1]
    pred_sq = jnp.sum(predicted * predicted, axis=1)
    pred_gain = jnp.sum(predicted * gain_cols, axis=1)
    pred_shift = jnp.sum(predicted * shift_cols, axis=1)
    scaled_in = to_core(scaled)
    resid = both(r_all[:half], r_in, 1).astype(f32) + biases[0]

    target = sums[0] + resid
    for a in arrived:
        target = target + a.astype(f32)
    own_sums = jnp.stack(
        [
            jnp.sum(predicted * target, axis=1),
            jnp.sum(target * target, axis=1),
            jnp.sum(target * gain_cols, axis=1),
            jnp.sum(target * shift_cols, axis=1),
            pred_sq,
            pred_gain,
            pred_shift,
            jnp.zeros_like(pred_sq),
        ]
    )
    groups = [list(range(c, 2 * CHIPS, 2)) for c in range(2)]
    totals = jnp.sum(
        lax.all_to_all(
            jnp.broadcast_to(own_sums[None], (CHIPS, *own_sums.shape)),
            "tensor",
            0,
            0,
            axis_index_groups=groups,
        ),
        axis=0,
    )
    cross_sum, targ_sq, targ_gain, targ_shift, pred_sq, pred_gain, pred_shift, _ = totals
    pred_inv = lax.rsqrt(pred_sq + epsilon)
    targ_inv = lax.rsqrt(targ_sq + epsilon)
    cosine = cross_sum * pred_inv * targ_inv
    a_row = pred_inv * targ_inv
    b_row = cosine * pred_inv * pred_inv
    loss_part = jnp.sum(1.0 - cosine)
    pred_grad = (
        -LOSS_SCALE * (target * a_row[:, None] - b_row[:, None] * predicted)
    ).astype(bf16)
    first_sum = -LOSS_SCALE * (a_row * targ_gain - b_row * pred_gain)
    second_sum = -LOSS_SCALE * (
        cosine * epsilon * pred_inv * pred_inv - (a_row * targ_shift - b_row * pred_shift)
    )

    pg_mine = own_cols(pred_grad, cols_own)
    pg_in = to_core(own_cols(pred_grad, cols_own, 1 - core))
    parts = back(order, pred_grad, weight)
    d_arrived = [to_chip(s, dx, dy) for s, (dx, dy) in zip(parts[1:], OFFSETS[1:], strict=True)]

    weight_part = dot(scaled, pg_mine, ((0,), (0,))) + dot(scaled_in, pg_in, ((0,), (0,)))
    bias_part = jnp.sum(pg_mine.astype(f32), axis=0) + jnp.sum(pg_in.astype(f32), axis=0)
    piece = full_width // (YL * Z)
    weight_part = weight_part.reshape(YL, Z, piece, cols_own)
    half_out = lax.dynamic_index_in_dim(weight_part, 1 - yl, 0, False).astype(bf16)
    half_in = to_batch(half_out, 1, 0)
    half_sum = (
        lax.dynamic_index_in_dim(weight_part, yl, 0, False) + half_in.astype(f32)
    ).astype(bf16)
    block = lax.dynamic_index_in_dim(half_sum, z, 0, False).astype(f32)
    for dz in range(1, Z):
        block = block + to_batch(
            lax.dynamic_index_in_dim(half_sum, (z + dz) % Z, 0, False), 0, dz
        ).astype(f32)
    block = block.astype(bf16)
    z_blocks = jnp.stack([block] + [to_batch(block, 0, dz) for dz in range(1, Z)])
    z_blocks = jnp.take(z_blocks, (z - jnp.arange(Z)) % Z, axis=0).reshape(Z * piece, cols_own)
    y_blocks = to_batch(z_blocks, 1, 0)
    grad_head_weight = jnp.where(
        yl == 0,
        jnp.concatenate([z_blocks, y_blocks], 0),
        jnp.concatenate([y_blocks, z_blocks], 0),
    ).astype(f32)

    dscaled = parts[0]
    for a in d_arrived:
        dscaled = dscaled + a.astype(f32)
    gain_chip = lax.dynamic_slice_in_dim(norm_gain, chip * feat_chip, feat_chip, 0)
    normed_chip = (f_chip.astype(f32) - row_mean[:, None]) * inv_std[:, None]
    dnormed = dscaled * gain_chip
    feat_grad = (
        inv_std[:, None]
        * (dnormed - first_sum[:, None] / full_width - normed_chip * (second_sum[:, None] / full_width))
    ).astype(bf16)
    gain_part = jnp.sum(dscaled * normed_chip, axis=0)
    shift_part = jnp.sum(dscaled, axis=0)
    fg_in = to_core(own_cols(feat_grad, feat_own, 1 - core))
    fg = jnp.concatenate([own_cols(feat_grad, feat_own), fg_in], 0)
    one_hot = (lax.broadcasted_iota(jnp.int32, (patches, masked), 0) == mask).astype(bf16)
    grad_student = dot(one_hot, fg, ((1,), (0,))).astype(bf16)
    norm_parts = jnp.stack([gain_part, shift_part])
    norm_in = to_core(own_cols(norm_parts, feat_own, 1 - core))
    norm_parts = (own_cols(norm_parts, feat_own) + norm_in).reshape(-1)
    small = jnp.concatenate([bias_part, norm_parts, jnp.full((96,), loss_part)])
    small = jnp.sum(
        lax.all_to_all(
            jnp.broadcast_to(small[None], (YL * Z, small.shape[0])), "batch", 0, 0
        ),
        axis=0,
    )
    grad_head_bias = small[:cols_own]
    grad_gain = small[cols_own : cols_own + feat_own]
    grad_shift = small[cols_own + feat_own : cols_own + 2 * feat_own]
    loss = (small[-1] + to_core(small[-1])) / (masked * YL * Z)
    return (loss, grad_student, grad_head_weight, grad_head_bias, grad_gain, grad_shift)


def solution(mesh):
    return jax.shard_map(
        on_device,
        mesh=mesh,
        in_specs=(
            P("batch", "tensor"),
            P("tensor", None),
            P("tensor"),
            P("batch", "tensor"),
            P("batch", "tensor"),
            P(),
            P(),
            P(None, "tensor"),
            P("tensor"),
            P("batch", None),
        ),
        out_specs=(
            P(),
            P("batch", "tensor"),
            P(None, "tensor"),
            P("tensor"),
            P("tensor"),
            P("tensor"),
        ),
        check_vma=False,
    )
```

```python
import functools

import jax
import jax.numpy as jnp
from jax import lax
from jax.experimental import pallas as pl
from jax.experimental.pallas import tpu as pltpu
from jax.sharding import PartitionSpec as P

LOSS_SCALE = 1024
epsilon = 1e-06
X, YH, YL, Z = 4, 2, 2, 8
CHIPS = X * YH
bf16, f32 = jnp.bfloat16, jnp.float32
VMEM = pl.BlockSpec(memory_space=pltpu.VMEM)
SMEM = pl.BlockSpec(memory_space=pltpu.SMEM)
HBM = pl.BlockSpec(memory_space=pl.ANY)
ANY = pl.BlockSpec()


def to_tensor(a, flip):
    return lax.ppermute(a, "tensor", [(t, t ^ flip) for t in range(2 * CHIPS)])


def to_batch(a, flip):
    return lax.ppermute(a, "batch", [(t, t ^ flip) for t in range(YL * Z)])


def to_core(a):
    return to_tensor(a, 1)


def dot(a, b, over_a=1, over_b=0):
    return lax.dot_general(
        a, b, (((over_a,), (over_b,)), ((), ())), preferred_element_type=f32
    )


def shape(dims, dtype):
    return jax.ShapeDtypeStruct(dims, dtype)


def call(kernel, out_shape, in_specs, scratch=(), limit=32, flops=0, moved=0, out_spec=VMEM):
    return pl.pallas_call(
        kernel,
        out_shape=out_shape,
        in_specs=in_specs,
        out_specs=jax.tree.map(lambda _: out_spec, out_shape),
        scratch_shapes=scratch,
        compiler_params=pltpu.CompilerParams(vmem_limit_bytes=limit << 20),
        cost_estimate=pl.CostEstimate(flops=flops, bytes_accessed=moved, transcendentals=0),
    )


def flipped(row):
    return jnp.broadcast_to(row, (128, row.shape[1])).T[:, :1]


def prepare_kernel(place_ref, own_ref, in_ref, gain_ref, shift_ref, bias_ref, cols_ref, gain_cols, shift_cols):
    size = own_ref.shape[0]
    for ref, half in ((own_ref, place_ref[0]), (in_ref, 1 - place_ref[0])):
        cols_ref[pl.ds(pl.multiple_of(half * size, size), size), :] = ref[...]
    weight = cols_ref[...].astype(f32)
    gain_cols[...] = jnp.sum(weight * gain_ref[...], axis=1, keepdims=True)
    shift_cols[...] = jnp.sum(weight * shift_ref[...], axis=1, keepdims=True) + flipped(bias_ref[1:2, :])


def forward_kernel(*refs):
    place_ref, f_own, f_in, r_mine, r_in, gain_ref, shift_ref, w_ref, bias_ref, gain_cols, shift_cols, *refs = refs
    scaled_ref, turned_ref, pred_ref, base_ref, known_ref, feat_ref = refs
    size = feat_ref.shape[0] // CHIPS
    for ref, y in ((f_own, place_ref[1]), (f_in, 1 - place_ref[1])):
        for i, chip in enumerate((0, 4, 2, 6)):
            at = pl.ds(pl.multiple_of((chip + y) * size, size), size)
            feat_ref[at, :] = ref[i * size : (i + 1) * size, :]
    feats = feat_ref[...].astype(f32)
    row_mean = jnp.mean(feats, axis=0, keepdims=True)
    variance = jnp.mean(feats * feats, axis=0, keepdims=True) - row_mean * row_mean
    inv_std = lax.rsqrt(variance + epsilon)
    normed = (feats - row_mean) * inv_std
    scaled_ref[...] = (normed * flipped(gain_ref[...]) + flipped(shift_ref[...])).astype(bf16)
    rows = scaled_ref.shape[1]
    turned_ref[...] = jnp.concatenate([scaled_ref[...], jnp.zeros((scaled_ref.shape[0], -rows % 128), bf16)], 1).T[:rows]
    predicted = dot(w_ref[...], scaled_ref[...]) + flipped(bias_ref[1:2, :])
    pred_ref[...] = predicted
    known_ref[0:1, :] = row_mean
    known_ref[1:2, :] = inv_std
    known_ref[2:4, :] = jnp.zeros((2, row_mean.shape[1]), f32)
    for i, with_this in enumerate((predicted, gain_cols[...], shift_cols[...])):
        known_ref[4 + i : 5 + i, :] = jnp.sum(predicted * with_this, axis=0, keepdims=True)
    known_ref[7:8, :] = jnp.zeros((1, row_mean.shape[1]), f32)
    own = r_mine.shape[0]
    for ref, half in ((r_mine, place_ref[0]), (r_in, 1 - place_ref[0])):
        base_ref[pl.ds(pl.multiple_of(half * own, own), own), :] = ref[...].astype(f32)
    base_ref[...] = base_ref[...] + flipped(bias_ref[0:1, :])


def target_kernel(*refs):
    blocks, refs = refs[:CHIPS], refs[CHIPS:]
    base_ref, pred_ref, gain_ref, shift_ref, known_ref, target_ref, sums_ref, block_ref, sems = refs
    copies = [pltpu.make_async_copy(b, block_ref.at[i], sems.at[i]) for i, b in enumerate(blocks[1:])]
    for copy in copies:
        copy.start()
    total = blocks[0][...]
    for i, copy in enumerate(copies):
        copy.wait()
        total = total + block_ref[i].astype(f32)
    rows = total.shape[0]
    total = jnp.concatenate([total, jnp.zeros((-rows % 128, total.shape[1]), f32)], 0)
    target = total.T[:, :rows] + base_ref[...]
    target_ref[...] = target
    predicted = pred_ref[...]
    for i, with_this in enumerate((predicted, target, gain_ref[...], shift_ref[...])):
        sums_ref[i : i + 1, :] = jnp.sum(target * with_this, axis=0, keepdims=True)
    sums_ref[4:8, :] = known_ref[4:8, :]


def grad_kernel(place_ref, sums_ref, target_ref, pred_ref, pg_ref, mine_ref, send_ref, rows_ref):
    totals = jnp.sum(sums_ref[...], axis=0)
    cross_sum, targ_sq, targ_gain, targ_shift, pred_sq, pred_gain, pred_shift = [
        totals[i : i + 1, :] for i in range(7)
    ]
    pred_inv = lax.rsqrt(pred_sq + epsilon)
    targ_inv = lax.rsqrt(targ_sq + epsilon)
    cosine = cross_sum * pred_inv * targ_inv
    a_row = pred_inv * targ_inv
    b_row = cosine * pred_inv * pred_inv
    pg_ref[...] = (-LOSS_SCALE * (target_ref[...] * a_row - b_row * pred_ref[...])).astype(bf16)
    own = mine_ref.shape[0]
    mine_ref[...] = pg_ref[pl.ds(pl.multiple_of(place_ref[0] * own, own), own), :]
    send_ref[...] = pg_ref[pl.ds(pl.multiple_of((1 - place_ref[0]) * own, own), own), :]
    rows_ref[0:1, :] = -LOSS_SCALE * (a_row * targ_gain - b_row * pred_gain)
    rows_ref[1:2, :] = -LOSS_SCALE * (
        cosine * epsilon * pred_inv * pred_inv - (a_row * targ_shift - b_row * pred_shift)
    )
    rows_ref[2:3, :] = 1.0 - cosine
    rows_ref[3:8, :] = jnp.zeros((5, totals.shape[1]), f32)


def on_device(
    teacher_hidden,
    teacher_down,
    teacher_bias,
    teacher_resid,
    student_feat,
    norm_gain,
    norm_shift,
    head_weight,
    head_bias,
    mask_index,
):
    masked = mask_index.shape[1]
    half = masked // 2
    patches, depth = teacher_hidden.shape
    feat_own = student_feat.shape[1]
    full_width, cols_own = head_weight.shape
    feat_chip, cols = 2 * feat_own, 2 * cols_own
    t = lax.axis_index("tensor")
    b = lax.axis_index("batch")
    core, yh, x = t & 1, (t >> 1) & 1, t >> 2
    yl, z = b // Z, b % Z
    place = jnp.stack([core, yh, x, yl, z]).astype(jnp.int32)

    def in_order(bit, mine, other, axis=0):
        return jnp.where(
            bit == 0,
            jnp.concatenate([mine, other], axis),
            jnp.concatenate([other, mine], axis),
        )

    def four_in_order(index, blocks):
        low = [jnp.where(index & 1 == 0, blocks[i], blocks[i ^ 1]) for i in range(4)]
        return [jnp.where(index & 2 == 0, low[i], low[i ^ 2]) for i in range(4)]

    w_own = head_weight.T
    w_in = to_core(w_own)
    bias_own = jnp.stack([teacher_bias, head_bias])
    bias_in = to_core(bias_own)
    mine, other = [
        lax.dynamic_slice_in_dim(mask_index, (core ^ i) * half, half, 1) for i in range(2)
    ]
    at = lax.broadcasted_iota(jnp.int32, (patches, half), 0)
    hot_mine, hot_other = lax.optimization_barrier(((at == mine).astype(bf16), (at == other).astype(bf16)))
    f_in = to_core(dot(student_feat.T, hot_other).astype(bf16))
    r_in = to_core(dot(teacher_resid.T, hot_other).astype(bf16))
    f_mine = dot(student_feat.T, hot_mine).astype(bf16)
    r_mine = dot(teacher_resid.T, hot_mine).astype(bf16)
    f_chip = in_order(core, f_mine, f_in)

    h_other = dot(hot_other, teacher_hidden, 0, 0).astype(bf16)
    h_other, f_chip = lax.optimization_barrier((h_other, f_chip))
    part_in = to_core(dot(h_other, teacher_down).astype(bf16))
    f_half = in_order(x >> 1, f_chip, to_tensor(f_chip, 8))
    h_mine = dot(hot_mine, teacher_hidden, 0, 0).astype(bf16)
    h_mine, w_in, r_in, bias_in, f_half = lax.optimization_barrier((h_mine, w_in, r_in, bias_in, f_half))
    part_own = dot(h_mine, teacher_down).astype(bf16)

    def both_parts(flip):
        start = ((t >> 1) ^ flip) * cols
        own, arrived = [lax.dynamic_slice_in_dim(a, start, cols, 1).astype(f32) for a in (part_own, part_in)]
        return own + arrived

    sums = {0: both_parts(0)}
    arrived = []
    for k in (4, 5, 6, 7, 2, 3, 1):
        sums[k] = both_parts(k).astype(bf16)
        arrived.append(to_tensor(sums[k], 2 * k))
    f_own = in_order(x & 1, f_half, to_tensor(f_half, 4))
    f_from = to_tensor(f_own, 2)

    (w_own, w_in, f_from), _ = lax.optimization_barrier(((w_own, w_in, f_from), arrived[0]))
    gain, shift = norm_gain[None], norm_shift[None]
    biases = in_order(core, bias_own, bias_in, 1)
    w_cols, gain_cols, shift_cols = call(
        prepare_kernel,
        [
            shape((cols, full_width), bf16),
            shape((cols, 1), f32),
            shape((cols, 1), f32),
        ],
        [SMEM, ANY, ANY, VMEM, VMEM, VMEM],
        flops=4 * cols * full_width,
        moved=6 * cols * full_width,
    )(place, w_own, w_in, gain, shift, biases)
    scaled, scaled_rows, predicted, base, known = call(
        forward_kernel,
        [
            shape((full_width, half), bf16),
            shape((half, full_width), bf16),
            shape((cols, half), f32),
            shape((cols, half), f32),
            shape((8, half), f32),
        ],
        [SMEM] + [ANY] * 4 + [VMEM] * 6,
        [pltpu.VMEM((full_width, half), bf16)],
        flops=2 * cols * full_width * half,
        moved=8 * cols * full_width,
    )(place, f_own, f_from, r_mine, r_in, gain, shift, w_cols, biases, gain_cols, shift_cols)
    row_mean, inv_std = known[0:1], known[1:2]
    gain_chip = lax.dynamic_slice_in_dim(norm_gain, (t >> 1) * feat_chip, feat_chip, 0)[:, None]
    normed_chip = (f_chip.astype(f32) - row_mean) * inv_std
    normed_chip, gain_chip, known = lax.optimization_barrier((normed_chip, gain_chip, known))

    target, own_sums = call(
        target_kernel,
        [shape((cols, half), f32), shape((8, half), f32)],
        [ANY] + [HBM] * (CHIPS - 1) + [VMEM] * 5,
        [pltpu.VMEM((CHIPS - 1, half, cols), bf16), pltpu.SemaphoreType.DMA((CHIPS - 1,))],
        flops=20 * half * cols,
        moved=24 * half * cols,
    )(sums[0], *arrived, base, predicted, gain_cols, shift_cols, known)
    scaled_rows, _ = lax.optimization_barrier((scaled_rows, own_sums))
    scaled_in = to_core(scaled_rows)
    groups = [list(range(c, 2 * CHIPS, 2)) for c in range(2)]
    all_sums = lax.all_to_all(
        jnp.broadcast_to(own_sums[None], (CHIPS, *own_sums.shape)),
        "tensor",
        0,
        0,
        axis_index_groups=groups,
    )
    pred_grad, pg_mine, pg_send, rows = call(
        grad_kernel,
        [
            shape((cols, half), bf16),
            shape((cols_own, half), bf16),
            shape((cols_own, half), bf16),
            shape((8, half), f32),
        ],
        [SMEM, VMEM, VMEM, VMEM],
        flops=6 * half * cols,
        moved=10 * half * cols,
    )(place, all_sums, target, predicted)
    pg_in = to_core(pg_send)
    part_a, part_b = 192, 64
    width = full_width // 2
    weight_part = dot(pg_mine, scaled, 1, 1) + dot(pg_in, scaled_in)
    bias_part = jnp.sum(pg_mine.astype(f32), axis=1) + jnp.sum(pg_in.astype(f32), axis=1)

    def part_of(y_half, z_half):
        return (
            lax.dynamic_slice(weight_part, (0, y_half * width), (part_a, width)),
            lax.dynamic_slice(weight_part, (part_a + z_half * part_b, 0), (part_b, full_width)),
        )

    a_keep, b_keep = part_of(yl, z & 1)
    a_send, b_send = [a.astype(bf16) for a in part_of(1 - yl, 1 - (z & 1))]
    pred_grad, _ = lax.optimization_barrier((pred_grad, a_send))
    d_part = dot(w_cols, pred_grad, 0, 0).astype(bf16)
    d_parts = lax.all_to_all(
        d_part.reshape(CHIPS, feat_chip, half), "tensor", 0, 0, axis_index_groups=groups
    )
    z0, zg = z & 1, z >> 1
    a_sum = a_keep + to_batch(a_send, YL * Z // 2).astype(f32)
    b_sum = b_keep + to_batch(b_send, 1).astype(f32)
    a_half, b_half = part_a // 2, width

    def rows_at(a, index, size):
        return lax.dynamic_slice_in_dim(a, index * size, size, 0)

    a_out = rows_at(a_sum, 1 - z0, a_half).astype(bf16)
    b_out = lax.dynamic_slice_in_dim(b_sum, (1 - yl) * width, width, 1).astype(bf16)
    a_sum = rows_at(a_sum, z0, a_half) + to_batch(a_out, 1).astype(f32)
    b_sum = lax.dynamic_slice_in_dim(b_sum, yl * width, width, 1) + to_batch(
        b_out, YL * Z // 2
    ).astype(f32)
    a_size, b_size = a_half // 4, part_b // 4

    def block_of(group):
        return jnp.concatenate([rows_at(a_sum, group, a_size), rows_at(b_sum, group, b_size)], 0)

    out_blocks = [block_of(zg ^ k).astype(bf16) for k in (1, 2, 3)]

    d_parts, _ = lax.optimization_barrier((d_parts, out_blocks))
    dscaled = jnp.sum(d_parts.astype(f32), axis=0)
    dnormed = dscaled * gain_chip
    feat_grad = (
        inv_std * (dnormed - rows[0:1] / full_width - normed_chip * (rows[1:2] / full_width))
    ).astype(bf16)
    norm_parts = jnp.stack([jnp.sum(dscaled * normed_chip, axis=1), jnp.sum(dscaled, axis=1)])
    fg_in = to_core(rows_at(feat_grad, 1 - core, feat_own))
    norm_out = lax.dynamic_slice_in_dim(norm_parts, (1 - core) * feat_own, feat_own, 1)
    norm_own = lax.dynamic_slice_in_dim(norm_parts, core * feat_own, feat_own, 1)
    loss_part = jnp.full((1,), jnp.sum(rows[2]))
    small_in = to_core(jnp.concatenate([norm_out.reshape(-1), loss_part]))
    small = jnp.concatenate([norm_own.reshape(-1), loss_part]) + small_in
    small = jnp.concatenate([small, bias_part, jnp.zeros((width - small.shape[0] - cols_own,), f32)])

    def with_small(a, small):
        high = lax.reduce_precision(small, 8, 7)
        middle = lax.reduce_precision(small - high, 8, 7)
        terms = jnp.stack([high, middle, small - high - middle]).astype(bf16)
        return jnp.concatenate([a, terms, jnp.zeros((5, width), bf16)], 0)

    def small_of(a):
        return jnp.sum(a[-8:].astype(f32), axis=0)

    block = block_of(zg)
    for k, out in zip((1, 2, 3), out_blocks, strict=True):
        block = block + to_batch(out, 2 * k).astype(f32)
    block = with_small(block.astype(bf16), small)
    got = [to_batch(block, 2 * k) for k in (1, 2, 3)]
    for g in got:
        small = small + small_of(g)
    out_blocks = four_in_order(zg, [block] + got)
    a_all = jnp.concatenate([o[:a_size] for o in out_blocks], 0)
    b_all = jnp.concatenate([o[a_size:-8] for o in out_blocks], 0)
    a_in = to_batch(with_small(a_all, small), 1)
    b_in = to_batch(b_all, YL * Z // 2)
    small = small + small_of(a_in)
    a_all = in_order(z0, a_all, a_in[:-8])
    b_all = in_order(yl, b_all, b_in, 1)
    a_in = to_batch(with_small(a_all, small), YL * Z // 2)
    b_in = to_batch(b_all, 1)
    small = small + small_of(a_in)
    a_all = in_order(yl, a_all, a_in[:-8], 1)
    b_all = in_order(z0, b_all, b_in)
    grad_head_weight = jnp.concatenate([a_all, b_all], 0).astype(f32).T
    hot = [
        (lax.broadcasted_iota(jnp.int32, (half, patches), 1) == mask_index[0, i * half : (i + 1) * half, None]).astype(bf16)
        for i in range(2)
    ]
    fg = in_order(core, rows_at(feat_grad, core, feat_own), fg_in, 1)
    grad_student = dot(fg, jnp.concatenate(hot, 0)).astype(bf16).T
    grad_gain = small[:feat_own]
    grad_shift = small[feat_own : 2 * feat_own]
    loss = small[2 * feat_own] / (masked * YL * Z)
    grad_head_bias = small[2 * feat_own + 1 : 2 * feat_own + 1 + cols_own]
    return (loss, grad_student, grad_head_weight, grad_head_bias, grad_gain, grad_shift)


def solution(mesh):
    return jax.shard_map(
        on_device,
        mesh=mesh,
        in_specs=(
            P("batch", "tensor"),
            P("tensor", None),
            P("tensor"),
            P("batch", "tensor"),
            P("batch", "tensor"),
            P(),
            P(),
            P(None, "tensor"),
            P("tensor"),
            P("batch", None),
        ),
        out_specs=(
            P(),
            P("batch", "tensor"),
            P(None, "tensor"),
            P("tensor"),
            P("tensor"),
            P("tensor"),
        ),
        check_vma=False,
    )
```

```python
import functools

import jax
import jax.numpy as jnp
from jax import lax
from jax.experimental import pallas as pl
from jax.experimental.pallas import tpu as pltpu
from jax.sharding import PartitionSpec as P

LOSS_SCALE = 1024
epsilon = 1e-06
X, YH, YL, Z = 4, 2, 2, 8
CHIPS = X * YH
bf16, f32 = jnp.bfloat16, jnp.float32
VMEM = pl.BlockSpec(memory_space=pltpu.VMEM)
SMEM = pl.BlockSpec(memory_space=pltpu.SMEM)
HBM = pl.BlockSpec(memory_space=pl.ANY)
ANY = pl.BlockSpec()


def to_tensor(a, flip):
    return lax.ppermute(a, "tensor", [(t, t ^ flip) for t in range(2 * CHIPS)])


def to_batch(a, flip):
    return lax.ppermute(a, "batch", [(t, t ^ flip) for t in range(YL * Z)])


def to_core(a):
    return to_tensor(a, 1)


def dot(a, b, over_a=1, over_b=0):
    return lax.dot_general(
        a, b, (((over_a,), (over_b,)), ((), ())), preferred_element_type=f32
    )


def shape(dims, dtype):
    return jax.ShapeDtypeStruct(dims, dtype)


def call(kernel, out_shape, in_specs, scratch=(), limit=32, flops=0, moved=0, out_spec=VMEM):
    return pl.pallas_call(
        kernel,
        out_shape=out_shape,
        in_specs=in_specs,
        out_specs=jax.tree.map(lambda _: out_spec, out_shape),
        scratch_shapes=scratch,
        compiler_params=pltpu.CompilerParams(vmem_limit_bytes=limit << 20),
        cost_estimate=pl.CostEstimate(flops=flops, bytes_accessed=moved, transcendentals=0),
    )


def gather_kernel(core_ref, mask_hbm, feat_hbm, hidden_hbm, resid_hbm, *refs):
    outs, (mask_ref, feat_ref, hidden_ref, resid_ref, sems) = refs[:6], refs[6:]
    pairs = ((mask_hbm, mask_ref), (feat_hbm, feat_ref), (hidden_hbm, hidden_ref), (resid_hbm, resid_ref))
    copies = [pltpu.make_async_copy(src, dst, sems.at[i]) for i, (src, dst) in enumerate(pairs)]
    for copy in copies:
        copy.start()
    copies[0].wait()
    half = mask_ref.shape[1] // 2
    low, high = mask_ref[:, :half], mask_ref[:, half:]
    first = core_ref[0] == 0
    at = lax.broadcasted_iota(jnp.int32, (hidden_ref.shape[0], half), 0)
    hot = [
        (at == index).astype(f32).astype(bf16)
        for index in (jnp.where(first, high, low), jnp.where(first, low, high))
    ]
    for copy, ref, place in zip(copies[1:], (feat_ref, hidden_ref, resid_ref), range(3), strict=True):
        copy.wait()
        for i in range(2):
            if place == 1:
                outs[3 * i + place][...] = dot(hot[i], ref[...], 0, 0).astype(bf16)
            else:
                outs[3 * i + place][...] = dot(ref[...], hot[i]).astype(bf16)


def flipped(row):
    return jnp.broadcast_to(row, (128, row.shape[1])).T[:, :1]


def prepare_kernel(place_ref, own_ref, in_ref, gain_ref, shift_ref, bias_ref, cols_ref, gain_cols, shift_cols):
    size = own_ref.shape[0]
    for ref, half in ((own_ref, place_ref[0]), (in_ref, 1 - place_ref[0])):
        cols_ref[pl.ds(pl.multiple_of(half * size, size), size), :] = ref[...]
    weight = cols_ref[...].astype(f32)
    gain_cols[...] = jnp.sum(weight * gain_ref[...], axis=1, keepdims=True)
    shift_cols[...] = jnp.sum(weight * shift_ref[...], axis=1, keepdims=True) + flipped(bias_ref[1:2, :])


def forward_kernel(*refs):
    place_ref, f_own, f_in, r_mine, r_in, gain_ref, shift_ref, w_ref, bias_ref, gain_cols, shift_cols, *refs = refs
    scaled_ref, turned_ref, pred_ref, base_ref, known_ref, feat_ref = refs
    size = feat_ref.shape[0] // CHIPS
    for ref, y in ((f_own, place_ref[1]), (f_in, 1 - place_ref[1])):
        for i in range(X):
            at = pl.ds(pl.multiple_of(((place_ref[2] ^ i) * YH + y) * size, size), size)
            feat_ref[at, :] = ref[i * size : (i + 1) * size, :]
    feats = feat_ref[...].astype(f32)
    row_mean = jnp.mean(feats, axis=0, keepdims=True)
    variance = jnp.mean(feats * feats, axis=0, keepdims=True) - row_mean * row_mean
    inv_std = lax.rsqrt(variance + epsilon)
    normed = (feats - row_mean) * inv_std
    scaled_ref[...] = (normed * flipped(gain_ref[...]) + flipped(shift_ref[...])).astype(bf16)
    rows = scaled_ref.shape[1]
    turned_ref[...] = jnp.concatenate([scaled_ref[...], jnp.zeros((scaled_ref.shape[0], -rows % 128), bf16)], 1).T[:rows]
    predicted = dot(w_ref[...], scaled_ref[...]) + flipped(bias_ref[1:2, :])
    pred_ref[...] = predicted
    known_ref[0:1, :] = row_mean
    known_ref[1:2, :] = inv_std
    known_ref[2:4, :] = jnp.zeros((2, row_mean.shape[1]), f32)
    for i, with_this in enumerate((predicted, gain_cols[...], shift_cols[...])):
        known_ref[4 + i : 5 + i, :] = jnp.sum(predicted * with_this, axis=0, keepdims=True)
    known_ref[7:8, :] = jnp.zeros((1, row_mean.shape[1]), f32)
    own = r_mine.shape[0]
    for ref, half in ((r_mine, place_ref[0]), (r_in, 1 - place_ref[0])):
        base_ref[pl.ds(pl.multiple_of(half * own, own), own), :] = ref[...].astype(f32)
    base_ref[...] = base_ref[...] + flipped(bias_ref[0:1, :])


def target_kernel(*refs):
    blocks, refs = refs[: X + 1], refs[X + 1 :]
    base_ref, pred_ref, gain_ref, shift_ref, known_ref, target_ref, sums_ref, block_ref, sems = refs
    copies = [pltpu.make_async_copy(b, block_ref.at[i], sems.at[i]) for i, b in enumerate(blocks[1:])]
    for copy in copies:
        copy.start()
    total = blocks[0][...]
    for i, copy in enumerate(copies):
        copy.wait()
        total = total + block_ref[i].astype(f32)
    rows = total.shape[0]
    total = jnp.concatenate([total, jnp.zeros((-rows % 128, total.shape[1]), f32)], 0)
    target = total.T[:, :rows] + base_ref[...]
    target_ref[...] = target
    predicted = pred_ref[...]
    sums = [
        jnp.sum(target * with_this, axis=0, keepdims=True)
        for with_this in (predicted, target, gain_ref[...], shift_ref[...])
    ]
    sums = jnp.concatenate(sums + [known_ref[4:8, :]], 0)
    for chip in range(CHIPS):
        sums_ref[chip] = sums


def grad_kernel(place_ref, sums_ref, target_ref, pred_ref, pg_ref, mine_ref, send_ref, rows_ref):
    totals = jnp.sum(sums_ref[...], axis=0)
    cross_sum, targ_sq, targ_gain, targ_shift, pred_sq, pred_gain, pred_shift = [
        totals[i : i + 1, :] for i in range(7)
    ]
    pred_inv = lax.rsqrt(pred_sq + epsilon)
    targ_inv = lax.rsqrt(targ_sq + epsilon)
    cosine = cross_sum * pred_inv * targ_inv
    a_row = pred_inv * targ_inv
    b_row = cosine * pred_inv * pred_inv
    own, rows = mine_ref.shape
    pg_ref[:, :rows] = (-LOSS_SCALE * (target_ref[...] * a_row - b_row * pred_ref[...])).astype(bf16)
    pg_ref[:, rows:] = jnp.zeros((pg_ref.shape[0], pg_ref.shape[1] - rows), bf16)
    mine_ref[...] = pg_ref[pl.ds(pl.multiple_of(place_ref[0] * own, own), own), :rows]
    send_ref[...] = pg_ref[pl.ds(pl.multiple_of((1 - place_ref[0]) * own, own), own), :rows]
    rows_ref[0:1, :] = -LOSS_SCALE * (a_row * targ_gain - b_row * pred_gain)
    rows_ref[1:2, :] = -LOSS_SCALE * (
        cosine * epsilon * pred_inv * pred_inv - (a_row * targ_shift - b_row * pred_shift)
    )
    rows_ref[2:3, :] = 1.0 - cosine
    rows_ref[3:8, :] = jnp.zeros((5, totals.shape[1]), f32)


def on_device(
    teacher_hidden,
    teacher_down,
    teacher_bias,
    teacher_resid,
    student_feat,
    norm_gain,
    norm_shift,
    head_weight,
    head_bias,
    mask_index,
):
    masked = mask_index.shape[1]
    half = masked // 2
    patches, depth = teacher_hidden.shape
    feat_own = student_feat.shape[1]
    full_width, cols_own = head_weight.shape
    feat_chip, cols = 2 * feat_own, 2 * cols_own
    t = lax.axis_index("tensor")
    b = lax.axis_index("batch")
    core, yh, x = t & 1, (t >> 1) & 1, t >> 2
    yl, z = b // Z, b % Z
    place = jnp.stack([core, yh, x]).astype(jnp.int32)

    def in_order(bit, mine, other, axis=0):
        return jnp.where(
            bit == 0,
            jnp.concatenate([mine, other], axis),
            jnp.concatenate([other, mine], axis),
        )

    def rows_at(a, index, size):
        return lax.dynamic_slice_in_dim(a, index * size, size, 0)

    def four_in_order(index, blocks):
        low = [jnp.where(index & 1 == 0, blocks[i], blocks[i ^ 1]) for i in range(4)]
        return [jnp.where(index & 2 == 0, low[i], low[i ^ 2]) for i in range(4)]

    w_own = head_weight.T
    w_in = to_core(w_own)
    kinds = [shape(n, bf16) for n in ((feat_own, half), (half, depth), (cols_own, half))]
    f_other, h_other, r_other, f_mine, h_mine, r_mine = call(
        gather_kernel,
        [*kinds, *kinds],
        [SMEM] + [HBM] * 4,
        [
            pltpu.VMEM(mask_index.shape, jnp.int32),
            pltpu.VMEM((feat_own, patches), bf16),
            pltpu.VMEM((patches, depth), bf16),
            pltpu.VMEM((cols_own, patches), bf16),
            pltpu.SemaphoreType.DMA((4,)),
        ],
        limit=62,
        flops=2 * masked * patches * (feat_own + cols_own + depth),
        moved=2 * patches * (feat_own + cols_own + depth),
        out_spec=ANY,
    )(core[None], mask_index, student_feat.T, teacher_hidden, teacher_resid.T)
    f_in = to_core(f_other)
    f_chip = in_order(core, f_mine, f_in)

    h_other, f_chip, w_in = lax.optimization_barrier((h_other, f_chip, w_in))
    part_in = to_core(dot(h_other, teacher_down).astype(bf16))
    f_own = jnp.concatenate([f_chip] + [to_tensor(f_chip, 4 * k) for k in range(1, X)], 0)
    part_own = dot(h_mine, teacher_down).astype(bf16)
    gain, shift = norm_gain[None], norm_shift[None]
    part_own, part_in, f_own = lax.optimization_barrier((part_own, part_in, f_own))

    def both_parts(flip):
        start = ((t >> 1) ^ flip) * cols
        own, arrived = [lax.dynamic_slice_in_dim(a, start, cols, 1).astype(f32) for a in (part_own, part_in)]
        return own + arrived

    far = [both_parts(k).astype(bf16) for k in (5, 3, 7)]
    arrived = [to_tensor(a, 4 * k) for a, k in zip(far, (2, 1, 3), strict=True)]
    part_own, part_in, _ = lax.optimization_barrier((part_own, part_in, far))
    f_from = to_tensor(f_own, 2)
    near = [both_parts(k).astype(bf16) for k in (4, 2, 6)]
    near = [to_tensor(a, 4 * k) for a, k in zip(near, (2, 1, 3), strict=True)]
    across = both_parts(1)
    for a in arrived:
        across = across + a.astype(f32)
    near.append(to_tensor(across.astype(bf16), 2))
    own_block = both_parts(0)
    (f_from, w_own, w_in, r_other, bias_own), _ = lax.optimization_barrier(
        ((f_from, w_own, w_in, r_other, (teacher_bias, head_bias)), arrived)
    )
    bias_own = jnp.stack(bias_own)
    biases = in_order(core, bias_own, to_core(bias_own), 1)
    r_in = to_core(r_other)
    w_cols, gain_cols, shift_cols = call(
        prepare_kernel,
        [shape((cols, full_width), bf16), shape((cols, 1), f32), shape((cols, 1), f32)],
        [SMEM, ANY, ANY, VMEM, VMEM, VMEM],
        limit=24,
        flops=4 * cols * full_width,
        moved=6 * cols * full_width,
    )(place, w_own, w_in, gain, shift, biases)
    scaled, scaled_rows, predicted, base, known = call(
        forward_kernel,
        [
            shape((full_width, half), bf16),
            shape((half, full_width), bf16),
            shape((cols, half), f32),
            shape((cols, half), f32),
            shape((8, half), f32),
        ],
        [SMEM] + [ANY] * 4 + [VMEM] * 2 + [ANY] + [VMEM] * 3,
        [pltpu.VMEM((full_width, half), bf16)],
        limit=24,
        flops=2 * cols * full_width * half,
        moved=8 * cols * full_width,
    )(place, f_own, f_from, r_mine, r_in, gain, shift, w_cols, biases, gain_cols, shift_cols)
    row_mean, inv_std = known[0:1], known[1:2]
    gain_chip = lax.dynamic_slice_in_dim(norm_gain, (t >> 1) * feat_chip, feat_chip, 0)[:, None]
    normed_chip = (f_chip.astype(f32) - row_mean) * inv_std
    normed_chip, gain_chip, known = lax.optimization_barrier((normed_chip, gain_chip, known))

    target, own_sums = call(
        target_kernel,
        [shape((cols, half), f32), shape((CHIPS, 8, half), f32)],
        [ANY] + [HBM] * X + [VMEM] * 5,
        [pltpu.VMEM((X, half, cols), bf16), pltpu.SemaphoreType.DMA((X,))],
        limit=16,
        flops=20 * half * cols,
        moved=24 * half * cols,
    )(own_block, *near, base, predicted, gain_cols, shift_cols, known)
    scaled_rows, _ = lax.optimization_barrier((scaled_rows, own_sums))
    scaled_in = to_core(scaled_rows)
    groups = [list(range(c, 2 * CHIPS, 2)) for c in range(2)]
    all_sums = lax.all_to_all(own_sums, "tensor", 0, 0, axis_index_groups=groups)
    pred_grad, pg_mine, pg_send, rows = call(
        grad_kernel,
        [
            shape((cols, half + -half % 128), bf16),
            shape((cols_own, half), bf16),
            shape((cols_own, half), bf16),
            shape((8, half), f32),
        ],
        [SMEM, VMEM, VMEM, VMEM],
        limit=16,
        flops=6 * half * cols,
        moved=10 * half * cols,
    )(place, all_sums, target, predicted)
    pg_in = to_core(pg_send)
    part_a, part_b = 192, 64
    width = full_width // 2
    weight_part = dot(pg_mine, scaled, 1, 1) + dot(pg_in, scaled_in)
    bias_part = jnp.sum(pg_mine.astype(f32), axis=1) + jnp.sum(pg_in.astype(f32), axis=1)

    def part_of(y_half, z_half):
        return (
            lax.dynamic_slice(weight_part, (0, y_half * width), (part_a, width)),
            lax.dynamic_slice(weight_part, (part_a + z_half * part_b, 0), (part_b, full_width)),
        )

    a_keep, b_keep = part_of(yl, z & 1)
    a_send, b_send = [a.astype(bf16) for a in part_of(1 - yl, 1 - (z & 1))]
    pred_grad, _ = lax.optimization_barrier((pred_grad, (a_send, b_send)))
    d_part = dot(w_cols, pred_grad, 0, 0).astype(bf16)
    z0, zg = z & 1, z >> 1
    a_arrived, b_arrived = to_batch(a_send, YL * Z // 2), to_batch(b_send, 1)
    d_in = [to_tensor(rows_at(d_part, x ^ k, YH * feat_chip), 4 * k) for k in (2, 1, 3)]
    a_sum = a_keep + a_arrived.astype(f32)
    b_sum = b_keep + b_arrived.astype(f32)
    a_half, b_half = part_a // 2, width

    a_out = rows_at(a_sum, 1 - z0, a_half).astype(bf16)
    b_out = lax.dynamic_slice_in_dim(b_sum, (1 - yl) * width, width, 1).astype(bf16)
    a_sum = rows_at(a_sum, z0, a_half) + to_batch(a_out, 1).astype(f32)
    b_sum = lax.dynamic_slice_in_dim(b_sum, yl * width, width, 1) + to_batch(
        b_out, YL * Z // 2
    ).astype(f32)
    a_size, b_size = a_half // 4, part_b // 4

    def block_of(group):
        return jnp.concatenate([rows_at(a_sum, group, a_size), rows_at(b_sum, group, b_size)], 0)

    out_blocks = [block_of(zg ^ k).astype(bf16) for k in (1, 2, 3)]

    d_in, _ = lax.optimization_barrier((d_in, (a_out, b_out)))
    d_pair = rows_at(d_part, x, YH * feat_chip).astype(f32)
    for d in d_in:
        d_pair = d_pair + d.astype(f32)
    d_across = to_tensor(rows_at(d_pair, 1 - yh, feat_chip).astype(bf16), 2)
    d_across, _ = lax.optimization_barrier((d_across, out_blocks))
    dscaled = (rows_at(d_pair, yh, feat_chip) + d_across.astype(f32))[:, :half]
    dnormed = dscaled * gain_chip
    feat_grad = (
        inv_std * (dnormed - rows[0:1] / full_width - normed_chip * (rows[1:2] / full_width))
    ).astype(bf16)
    norm_parts = jnp.stack([jnp.sum(dscaled * normed_chip, axis=1), jnp.sum(dscaled, axis=1)])
    fg_in = to_core(rows_at(feat_grad, 1 - core, feat_own))
    norm_out = lax.dynamic_slice_in_dim(norm_parts, (1 - core) * feat_own, feat_own, 1)
    norm_own = lax.dynamic_slice_in_dim(norm_parts, core * feat_own, feat_own, 1)
    loss_part = jnp.full((1,), jnp.sum(rows[2]))
    small_in = to_core(jnp.concatenate([norm_out.reshape(-1), loss_part]))
    small = jnp.concatenate([norm_own.reshape(-1), loss_part]) + small_in
    small = jnp.concatenate([small, bias_part, jnp.zeros((width - small.shape[0] - cols_own,), f32)])

    def with_small(a, small):
        high = lax.reduce_precision(small, 8, 7)
        middle = lax.reduce_precision(small - high, 8, 7)
        terms = jnp.stack([high, middle, small - high - middle]).astype(bf16)
        return jnp.concatenate([a, terms, jnp.zeros((5, width), bf16)], 0)

    def small_of(a):
        return jnp.sum(a[-8:].astype(f32), axis=0)

    block = block_of(zg)
    for k, out in zip((1, 2, 3), out_blocks, strict=True):
        block = block + to_batch(out, 2 * k).astype(f32)
    block = with_small(block.astype(bf16), small)
    got = [to_batch(block, 2 * k) for k in (1, 2, 3)]
    for g in got:
        small = small + small_of(g)
    out_blocks = four_in_order(zg, [block] + got)
    a_all = jnp.concatenate([o[:a_size] for o in out_blocks], 0)
    b_all = jnp.concatenate([o[a_size:-8] for o in out_blocks], 0)
    a_in = to_batch(with_small(a_all, small), 1)
    b_in = to_batch(b_all, YL * Z // 2)
    small = small + small_of(a_in)
    a_all = in_order(z0, a_all, a_in[:-8])
    b_all = in_order(yl, b_all, b_in, 1)
    a_in = to_batch(with_small(a_all, small), YL * Z // 2)
    b_in = to_batch(b_all, 1)
    small = small + small_of(a_in)
    a_all = in_order(yl, a_all, a_in[:-8], 1)
    b_all = in_order(z0, b_all, b_in)
    grad_head_weight = jnp.concatenate([a_all, b_all], 0).astype(f32).T
    hot = [
        (lax.broadcasted_iota(jnp.int32, (half, patches), 1) == mask_index[0, i * half : (i + 1) * half, None]).astype(bf16)
        for i in range(2)
    ]
    fg = in_order(core, rows_at(feat_grad, core, feat_own), fg_in, 1)
    grad_student = dot(fg, jnp.concatenate(hot, 0)).astype(bf16).T
    grad_gain = small[:feat_own]
    grad_shift = small[feat_own : 2 * feat_own]
    loss = small[2 * feat_own] / (masked * YL * Z)
    grad_head_bias = small[2 * feat_own + 1 : 2 * feat_own + 1 + cols_own]
    return (loss, grad_student, grad_head_weight, grad_head_bias, grad_gain, grad_shift)


def solution(mesh):
    return jax.shard_map(
        on_device,
        mesh=mesh,
        in_specs=(
            P("batch", "tensor"),
            P("tensor", None),
            P("tensor"),
            P("batch", "tensor"),
            P("batch", "tensor"),
            P(),
            P(),
            P(None, "tensor"),
            P("tensor"),
            P("batch", None),
        ),
        out_specs=(
            P(),
            P("batch", "tensor"),
            P(None, "tensor"),
            P("tensor"),
            P("tensor"),
            P("tensor"),
        ),
        check_vma=False,
    )
```

```python
import functools

import jax
import jax.numpy as jnp
from jax import lax
from jax.experimental import pallas as pl
from jax.experimental.pallas import tpu as pltpu
from jax.sharding import PartitionSpec as P

LOSS_SCALE = 1024
epsilon = 1e-06
X, YH, YL, Z = 4, 2, 2, 8
CHIPS = X * YH
bf16, f32 = jnp.bfloat16, jnp.float32
VMEM = pl.BlockSpec(memory_space=pltpu.VMEM)
SMEM = pl.BlockSpec(memory_space=pltpu.SMEM)
HBM = pl.BlockSpec(memory_space=pl.ANY)
ANY = pl.BlockSpec()


def to_tensor(a, flip):
    return lax.ppermute(a, "tensor", [(t, t ^ flip) for t in range(2 * CHIPS)])


def to_batch(a, flip):
    return lax.ppermute(a, "batch", [(t, t ^ flip) for t in range(YL * Z)])


def to_core(a):
    return to_tensor(a, 1)


def dot(a, b, over_a=1, over_b=0):
    return lax.dot_general(
        a, b, (((over_a,), (over_b,)), ((), ())), preferred_element_type=f32
    )


def shape(dims, dtype):
    return jax.ShapeDtypeStruct(dims, dtype)


def call(kernel, out_shape, in_specs, scratch=(), limit=32, flops=0, moved=0, out_spec=VMEM):
    return pl.pallas_call(
        kernel,
        out_shape=out_shape,
        in_specs=in_specs,
        out_specs=jax.tree.map(lambda _: out_spec, out_shape),
        scratch_shapes=scratch,
        compiler_params=pltpu.CompilerParams(vmem_limit_bytes=limit << 20),
        cost_estimate=pl.CostEstimate(flops=flops, bytes_accessed=moved, transcendentals=0),
    )


def gather_kernel(core_ref, mask_hbm, feat_hbm, hidden_hbm, resid_hbm, *refs):
    outs, (mask_ref, feat_ref, hidden_ref, resid_ref, sems) = refs[:6], refs[6:]
    pairs = ((mask_hbm, mask_ref), (feat_hbm, feat_ref), (hidden_hbm, hidden_ref), (resid_hbm, resid_ref))
    copies = [pltpu.make_async_copy(src, dst, sems.at[i]) for i, (src, dst) in enumerate(pairs)]
    for copy in copies:
        copy.start()
    copies[0].wait()
    half = mask_ref.shape[1] // 2
    low, high = mask_ref[:, :half], mask_ref[:, half:]
    first = core_ref[0] == 0
    at = lax.broadcasted_iota(jnp.int32, (hidden_ref.shape[0], half), 0)
    hot = [
        (at == index).astype(f32).astype(bf16)
        for index in (jnp.where(first, high, low), jnp.where(first, low, high))
    ]
    for copy, ref, place in zip(copies[1:], (feat_ref, hidden_ref, resid_ref), range(3), strict=True):
        copy.wait()
        for i in range(2):
            if place == 1:
                outs[3 * i + place][...] = dot(hot[i], ref[...], 0, 0).astype(bf16)
            else:
                outs[3 * i + place][...] = dot(ref[...], hot[i]).astype(bf16)


def flipped(row):
    return jnp.broadcast_to(row, (128, row.shape[1])).T[:, :1]


def prepare_kernel(place_ref, own_ref, in_ref, gain_ref, shift_ref, bias_ref, cols_ref, gain_cols, shift_cols):
    size = own_ref.shape[0]
    for ref, half in ((own_ref, place_ref[0]), (in_ref, 1 - place_ref[0])):
        cols_ref[pl.ds(pl.multiple_of(half * size, size), size), :] = ref[...]
    weight = cols_ref[...].astype(f32)
    gain_cols[...] = jnp.sum(weight * gain_ref[...], axis=1, keepdims=True)
    shift_cols[...] = jnp.sum(weight * shift_ref[...], axis=1, keepdims=True) + flipped(bias_ref[1:2, :])


def forward_kernel(*refs):
    place_ref, f_own, f_in, r_mine, r_in, gain_ref, shift_ref, w_ref, bias_ref, gain_cols, shift_cols, *refs = refs
    scaled_ref, turned_ref, pred_ref, base_ref, known_ref, feat_ref = refs
    size = feat_ref.shape[0] // CHIPS
    for ref, y in ((f_own, place_ref[1]), (f_in, 1 - place_ref[1])):
        for i in range(X):
            at = pl.ds(pl.multiple_of(((place_ref[2] ^ i) * YH + y) * size, size), size)
            feat_ref[at, :] = ref[i * size : (i + 1) * size, :]
    feats = feat_ref[...].astype(f32)
    row_mean = jnp.mean(feats, axis=0, keepdims=True)
    variance = jnp.mean(feats * feats, axis=0, keepdims=True) - row_mean * row_mean
    inv_std = lax.rsqrt(variance + epsilon)
    normed = (feats - row_mean) * inv_std
    scaled_ref[...] = (normed * flipped(gain_ref[...]) + flipped(shift_ref[...])).astype(bf16)
    rows = scaled_ref.shape[1]
    turned_ref[...] = jnp.concatenate([scaled_ref[...], jnp.zeros((scaled_ref.shape[0], -rows % 128), bf16)], 1).T[:rows]
    predicted = dot(w_ref[...], scaled_ref[...]) + flipped(bias_ref[1:2, :])
    pred_ref[...] = predicted
    known_ref[0:1, :] = row_mean
    known_ref[1:2, :] = inv_std
    known_ref[2:4, :] = jnp.zeros((2, row_mean.shape[1]), f32)
    for i, with_this in enumerate((predicted, gain_cols[...], shift_cols[...])):
        known_ref[4 + i : 5 + i, :] = jnp.sum(predicted * with_this, axis=0, keepdims=True)
    known_ref[7:8, :] = jnp.zeros((1, row_mean.shape[1]), f32)
    own = r_mine.shape[0]
    for ref, half in ((r_mine, place_ref[0]), (r_in, 1 - place_ref[0])):
        base_ref[pl.ds(pl.multiple_of(half * own, own), own), :] = ref[...].astype(f32)
    base_ref[...] = base_ref[...] + flipped(bias_ref[0:1, :])


def target_kernel(*refs):
    blocks, refs = refs[: X + 1], refs[X + 1 :]
    base_ref, pred_ref, gain_ref, shift_ref, known_ref, target_ref, sums_ref, block_ref, sems = refs
    copies = [pltpu.make_async_copy(b, block_ref.at[i], sems.at[i]) for i, b in enumerate(blocks[1:])]
    for copy in copies:
        copy.start()
    total = blocks[0][...]
    for i, copy in enumerate(copies):
        copy.wait()
        total = total + block_ref[i].astype(f32)
    rows = total.shape[0]
    total = jnp.concatenate([total, jnp.zeros((-rows % 128, total.shape[1]), f32)], 0)
    target = total.T[:, :rows] + base_ref[...]
    target_ref[...] = target
    predicted = pred_ref[...]
    sums = [
        jnp.sum(target * with_this, axis=0, keepdims=True)
        for with_this in (predicted, target, gain_ref[...], shift_ref[...])
    ]
    sums = jnp.concatenate(sums + [known_ref[4:8, :]], 0)
    for chip in range(CHIPS):
        sums_ref[chip] = sums


def grad_kernel(place_ref, sums_ref, target_ref, pred_ref, pg_ref, mine_ref, send_ref, rows_ref):
    totals = jnp.sum(sums_ref[...], axis=0)
    cross_sum, targ_sq, targ_gain, targ_shift, pred_sq, pred_gain, pred_shift = [
        totals[i : i + 1, :] for i in range(7)
    ]
    pred_inv = lax.rsqrt(pred_sq + epsilon)
    targ_inv = lax.rsqrt(targ_sq + epsilon)
    cosine = cross_sum * pred_inv * targ_inv
    a_row = pred_inv * targ_inv
    b_row = cosine * pred_inv * pred_inv
    own, rows = mine_ref.shape
    pg_ref[:, :rows] = (-LOSS_SCALE * (target_ref[...] * a_row - b_row * pred_ref[...])).astype(bf16)
    pg_ref[:, rows:] = jnp.zeros((pg_ref.shape[0], pg_ref.shape[1] - rows), bf16)
    mine_ref[...] = pg_ref[pl.ds(pl.multiple_of(place_ref[0] * own, own), own), :rows]
    send_ref[...] = pg_ref[pl.ds(pl.multiple_of((1 - place_ref[0]) * own, own), own), :rows]
    rows_ref[0:1, :] = -LOSS_SCALE * (a_row * targ_gain - b_row * pred_gain)
    rows_ref[1:2, :] = -LOSS_SCALE * (
        cosine * epsilon * pred_inv * pred_inv - (a_row * targ_shift - b_row * pred_shift)
    )
    rows_ref[2:3, :] = 1.0 - cosine
    rows_ref[3:8, :] = jnp.zeros((5, totals.shape[1]), f32)


def on_device(
    teacher_hidden,
    teacher_down,
    teacher_bias,
    teacher_resid,
    student_feat,
    norm_gain,
    norm_shift,
    head_weight,
    head_bias,
    mask_index,
):
    masked = mask_index.shape[1]
    half = masked // 2
    patches, depth = teacher_hidden.shape
    feat_own = student_feat.shape[1]
    full_width, cols_own = head_weight.shape
    feat_chip, cols = 2 * feat_own, 2 * cols_own
    t = lax.axis_index("tensor")
    b = lax.axis_index("batch")
    core, yh, x = t & 1, (t >> 1) & 1, t >> 2
    yl, z = b // Z, b % Z
    place = jnp.stack([core, yh, x]).astype(jnp.int32)

    def in_order(bit, mine, other, axis=0):
        return jnp.where(
            bit == 0,
            jnp.concatenate([mine, other], axis),
            jnp.concatenate([other, mine], axis),
        )

    def rows_at(a, index, size):
        return lax.dynamic_slice_in_dim(a, index * size, size, 0)

    def four_in_order(index, blocks):
        low = [jnp.where(index & 1 == 0, blocks[i], blocks[i ^ 1]) for i in range(4)]
        return [jnp.where(index & 2 == 0, low[i], low[i ^ 2]) for i in range(4)]

    w_own = head_weight.T
    w_in = to_core(w_own)
    kinds = [shape(n, bf16) for n in ((feat_own, half), (half, depth), (cols_own, half))]
    f_other, h_other, r_other, f_mine, h_mine, r_mine = call(
        gather_kernel,
        [*kinds, *kinds],
        [SMEM] + [HBM] * 4,
        [
            pltpu.VMEM(mask_index.shape, jnp.int32),
            pltpu.VMEM((feat_own, patches), bf16),
            pltpu.VMEM((patches, depth), bf16),
            pltpu.VMEM((cols_own, patches), bf16),
            pltpu.SemaphoreType.DMA((4,)),
        ],
        limit=62,
        flops=2 * masked * patches * (feat_own + cols_own + depth),
        moved=2 * patches * (feat_own + cols_own + depth),
        out_spec=ANY,
    )(core[None], mask_index, student_feat.T, teacher_hidden, teacher_resid.T)
    f_in = to_core(f_other)
    f_chip = in_order(core, f_mine, f_in)

    h_other, f_chip, w_in = lax.optimization_barrier((h_other, f_chip, w_in))
    part_in = to_core(dot(h_other, teacher_down).astype(bf16))
    f_own = jnp.concatenate([f_chip] + [to_tensor(f_chip, 4 * k) for k in range(1, X)], 0)
    part_own = dot(h_mine, teacher_down).astype(bf16)
    gain, shift = norm_gain[None], norm_shift[None]
    part_own, part_in, f_own = lax.optimization_barrier((part_own, part_in, f_own))

    def both_parts(flip):
        start = ((t >> 1) ^ flip) * cols
        own, arrived = [lax.dynamic_slice_in_dim(a, start, cols, 1).astype(f32) for a in (part_own, part_in)]
        return own + arrived

    far = [both_parts(k).astype(bf16) for k in (5, 3, 7)]
    arrived = [to_tensor(a, 4 * k) for a, k in zip(far, (2, 1, 3), strict=True)]
    part_own, part_in, _ = lax.optimization_barrier((part_own, part_in, far))
    f_from = to_tensor(f_own, 2)
    near = [both_parts(k).astype(bf16) for k in (4, 2, 6)]
    near = [to_tensor(a, 4 * k) for a, k in zip(near, (2, 1, 3), strict=True)]
    across = both_parts(1)
    for a in arrived:
        across = across + a.astype(f32)
    near.append(to_tensor(across.astype(bf16), 2))
    own_block = both_parts(0)
    (f_from, w_own, w_in, r_other, bias_own), _ = lax.optimization_barrier(
        ((f_from, w_own, w_in, r_other, (teacher_bias, head_bias)), arrived)
    )
    bias_own = jnp.stack(bias_own)
    biases = in_order(core, bias_own, to_core(bias_own), 1)
    r_in = to_core(r_other)
    w_cols, gain_cols, shift_cols = call(
        prepare_kernel,
        [shape((cols, full_width), bf16), shape((cols, 1), f32), shape((cols, 1), f32)],
        [SMEM, ANY, ANY, VMEM, VMEM, VMEM],
        limit=24,
        flops=4 * cols * full_width,
        moved=6 * cols * full_width,
    )(place, w_own, w_in, gain, shift, biases)
    scaled, scaled_rows, predicted, base, known = call(
        forward_kernel,
        [
            shape((full_width, half), bf16),
            shape((half, full_width), bf16),
            shape((cols, half), f32),
            shape((cols, half), f32),
            shape((8, half), f32),
        ],
        [SMEM] + [ANY] * 4 + [VMEM] * 2 + [ANY] + [VMEM] * 3,
        [pltpu.VMEM((full_width, half), bf16)],
        limit=24,
        flops=2 * cols * full_width * half,
        moved=8 * cols * full_width,
    )(place, f_own, f_from, r_mine, r_in, gain, shift, w_cols, biases, gain_cols, shift_cols)
    row_mean, inv_std = known[0:1], known[1:2]
    gain_chip = lax.dynamic_slice_in_dim(norm_gain, (t >> 1) * feat_chip, feat_chip, 0)[:, None]
    normed_chip = (f_chip.astype(f32) - row_mean) * inv_std
    normed_chip, gain_chip, known = lax.optimization_barrier((normed_chip, gain_chip, known))

    target, own_sums = call(
        target_kernel,
        [shape((cols, half), f32), shape((CHIPS, 8, half), f32)],
        [ANY] + [HBM] * X + [VMEM] * 5,
        [pltpu.VMEM((X, half, cols), bf16), pltpu.SemaphoreType.DMA((X,))],
        limit=16,
        flops=20 * half * cols,
        moved=24 * half * cols,
    )(own_block, *near, base, predicted, gain_cols, shift_cols, known)
    scaled_rows, _ = lax.optimization_barrier((scaled_rows, own_sums))
    scaled_in = to_core(scaled_rows)
    groups = [list(range(c, 2 * CHIPS, 2)) for c in range(2)]
    all_sums = lax.all_to_all(own_sums, "tensor", 0, 0, axis_index_groups=groups)
    pred_grad, pg_mine, pg_send, rows = call(
        grad_kernel,
        [
            shape((cols, half + -half % 128), bf16),
            shape((cols_own, half), bf16),
            shape((cols_own, half), bf16),
            shape((8, half), f32),
        ],
        [SMEM, VMEM, VMEM, VMEM],
        limit=16,
        flops=6 * half * cols,
        moved=10 * half * cols,
    )(place, all_sums, target, predicted)
    pg_in = to_core(pg_send)
    part_a, part_b = 192, 64
    width = full_width // 2
    weight_part = dot(pg_mine, scaled, 1, 1) + dot(pg_in, scaled_in)
    bias_part = jnp.sum(pg_mine.astype(f32), axis=1) + jnp.sum(pg_in.astype(f32), axis=1)

    def part_of(y_half, z_half):
        return (
            lax.dynamic_slice(weight_part, (0, y_half * width), (part_a, width)),
            lax.dynamic_slice(weight_part, (part_a + z_half * part_b, 0), (part_b, full_width)),
        )

    a_keep, b_keep = part_of(yl, z & 1)
    a_send, b_send = [a.astype(bf16) for a in part_of(1 - yl, 1 - (z & 1))]
    pred_grad, _ = lax.optimization_barrier((pred_grad, (a_send, b_send)))
    d_part = dot(w_cols, pred_grad, 0, 0).astype(bf16)
    z0, zg = z & 1, z >> 1
    a_arrived, b_arrived = to_batch(a_send, YL * Z // 2), to_batch(b_send, 1)
    d_in = [to_tensor(rows_at(d_part, x ^ k, YH * feat_chip), 4 * k) for k in (2, 1, 3)]
    a_sum = a_keep + a_arrived.astype(f32)
    b_sum = b_keep + b_arrived.astype(f32)
    a_half, b_half = part_a // 2, width

    a_out = rows_at(a_sum, 1 - z0, a_half).astype(bf16)
    b_out = lax.dynamic_slice_in_dim(b_sum, (1 - yl) * width, width, 1).astype(bf16)
    a_sum = rows_at(a_sum, z0, a_half) + to_batch(a_out, 1).astype(f32)
    b_sum = lax.dynamic_slice_in_dim(b_sum, yl * width, width, 1) + to_batch(
        b_out, YL * Z // 2
    ).astype(f32)
    a_size, b_size = a_half // 4, part_b // 4

    def block_of(group):
        return jnp.concatenate([rows_at(a_sum, group, a_size), rows_at(b_sum, group, b_size)], 0)

    out_blocks = [block_of(zg ^ k).astype(bf16) for k in (1, 2, 3)]

    d_in, _ = lax.optimization_barrier((d_in, (a_out, b_out)))
    d_pair = rows_at(d_part, x, YH * feat_chip).astype(f32)
    for d in d_in:
        d_pair = d_pair + d.astype(f32)
    d_across = to_tensor(rows_at(d_pair, 1 - yh, feat_chip).astype(bf16), 2)
    d_across, _ = lax.optimization_barrier((d_across, out_blocks))
    dscaled = (rows_at(d_pair, yh, feat_chip) + d_across.astype(f32))[:, :half]
    dnormed = dscaled * gain_chip
    feat_grad = (
        inv_std * (dnormed - rows[0:1] / full_width - normed_chip * (rows[1:2] / full_width))
    ).astype(bf16)
    norm_parts = jnp.stack([jnp.sum(dscaled * normed_chip, axis=1), jnp.sum(dscaled, axis=1)])
    fg_in = to_core(rows_at(feat_grad, 1 - core, feat_own))
    norm_out = lax.dynamic_slice_in_dim(norm_parts, (1 - core) * feat_own, feat_own, 1)
    norm_own = lax.dynamic_slice_in_dim(norm_parts, core * feat_own, feat_own, 1)
    loss_part = jnp.full((1,), jnp.sum(rows[2]))
    small_in = to_core(jnp.concatenate([norm_out.reshape(-1), loss_part]))
    small = jnp.concatenate([norm_own.reshape(-1), loss_part]) + small_in
    small = jnp.concatenate([small, bias_part, jnp.zeros((width - small.shape[0] - cols_own,), f32)])

    def with_small(a, small):
        high = lax.reduce_precision(small, 8, 7)
        middle = lax.reduce_precision(small - high, 8, 7)
        terms = jnp.stack([high, middle, small - high - middle]).astype(bf16)
        return jnp.concatenate([a, terms, jnp.zeros((5, width), bf16)], 0)

    def small_of(a):
        return jnp.sum(a[-8:].astype(f32), axis=0)

    block = block_of(zg)
    for k, out in zip((1, 2, 3), out_blocks, strict=True):
        block = block + to_batch(out, 2 * k).astype(f32)
    block = with_small(block.astype(bf16), small)
    got = [to_batch(block, 2 * k) for k in (1, 2, 3)]
    parts = four_in_order(zg, [small_of(a) for a in [block] + got])
    small = (parts[0] + parts[1]) + (parts[2] + parts[3])
    out_blocks = four_in_order(zg, [block] + got)
    a_all = jnp.concatenate([o[:a_size] for o in out_blocks], 0)
    b_all = jnp.concatenate([o[a_size:-8] for o in out_blocks], 0)
    a_all = with_small(a_all, small)
    a_in = to_batch(a_all, 1)
    b_in = to_batch(b_all, YL * Z // 2)
    small = small_of(a_all) + small_of(a_in)
    a_all = in_order(z0, a_all[:-8], a_in[:-8])
    b_all = in_order(yl, b_all, b_in, 1)
    a_all = with_small(a_all, small)
    a_in = to_batch(a_all, YL * Z // 2)
    b_in = to_batch(b_all, 1)
    small = small_of(a_all) + small_of(a_in)
    a_all = in_order(yl, a_all[:-8], a_in[:-8], 1)
    b_all = in_order(z0, b_all, b_in)
    grad_head_weight = jnp.concatenate([a_all, b_all], 0).astype(f32).T
    hot = [
        (lax.broadcasted_iota(jnp.int32, (half, patches), 1) == mask_index[0, i * half : (i + 1) * half, None]).astype(bf16)
        for i in range(2)
    ]
    fg = in_order(core, rows_at(feat_grad, core, feat_own), fg_in, 1)
    grad_student = dot(fg, jnp.concatenate(hot, 0)).astype(bf16).T
    grad_gain = small[:feat_own]
    grad_shift = small[feat_own : 2 * feat_own]
    loss = small[2 * feat_own] / (masked * YL * Z)
    grad_head_bias = small[2 * feat_own + 1 : 2 * feat_own + 1 + cols_own]
    return (loss, grad_student, grad_head_weight, grad_head_bias, grad_gain, grad_shift)


def solution(mesh):
    return jax.shard_map(
        on_device,
        mesh=mesh,
        in_specs=(
            P("batch", "tensor"),
            P("tensor", None),
            P("tensor"),
            P("batch", "tensor"),
            P("batch", "tensor"),
            P(),
            P(),
            P(None, "tensor"),
            P("tensor"),
            P("batch", None),
        ),
        out_specs=(
            P(),
            P("batch", "tensor"),
            P(None, "tensor"),
            P("tensor"),
            P("tensor"),
            P("tensor"),
        ),
        check_vma=False,
    )
```

```python
import functools

import jax
import jax.numpy as jnp
from jax import lax
from jax.experimental import pallas as pl
from jax.experimental.pallas import tpu as pltpu
from jax.sharding import PartitionSpec as P

LOSS_SCALE = 1024
epsilon = 1e-06
X, YH, YL, Z = 4, 2, 2, 8
CHIPS = X * YH
bf16, f32 = jnp.bfloat16, jnp.float32
VMEM = pl.BlockSpec(memory_space=pltpu.VMEM)
SMEM = pl.BlockSpec(memory_space=pltpu.SMEM)
HBM = pl.BlockSpec(memory_space=pl.ANY)
ANY = pl.BlockSpec()


def to_tensor(a, flip):
    return lax.ppermute(a, "tensor", [(t, t ^ flip) for t in range(2 * CHIPS)])


def to_batch(a, flip):
    return lax.ppermute(a, "batch", [(t, t ^ flip) for t in range(YL * Z)])


def to_core(a):
    return to_tensor(a, 1)


def dot(a, b, over_a=1, over_b=0):
    return lax.dot_general(
        a, b, (((over_a,), (over_b,)), ((), ())), preferred_element_type=f32
    )


def shape(dims, dtype):
    return jax.ShapeDtypeStruct(dims, dtype)


def call(kernel, out_shape, in_specs, scratch=(), limit=32, flops=0, moved=0, out_spec=VMEM):
    return pl.pallas_call(
        kernel,
        out_shape=out_shape,
        in_specs=in_specs,
        out_specs=jax.tree.map(lambda _: out_spec, out_shape),
        scratch_shapes=scratch,
        compiler_params=pltpu.CompilerParams(vmem_limit_bytes=limit << 20),
        cost_estimate=pl.CostEstimate(flops=flops, bytes_accessed=moved, transcendentals=0),
    )


def gather_kernel(core_ref, mask_hbm, feat_hbm, hidden_hbm, resid_hbm, *refs):
    outs, (mask_ref, feat_ref, hidden_ref, resid_ref, sems) = refs[:6], refs[6:]
    pairs = ((mask_hbm, mask_ref), (feat_hbm, feat_ref), (hidden_hbm, hidden_ref), (resid_hbm, resid_ref))
    copies = [pltpu.make_async_copy(src, dst, sems.at[i]) for i, (src, dst) in enumerate(pairs)]
    for copy in copies:
        copy.start()
    copies[0].wait()
    half = mask_ref.shape[1] // 2
    low, high = mask_ref[:, :half], mask_ref[:, half:]
    first = core_ref[0] == 0
    at = lax.broadcasted_iota(jnp.int32, (hidden_ref.shape[0], half), 0)
    hot = [
        (at == index).astype(f32).astype(bf16)
        for index in (jnp.where(first, high, low), jnp.where(first, low, high))
    ]
    for copy, ref, place in zip(copies[1:], (feat_ref, hidden_ref, resid_ref), range(3), strict=True):
        copy.wait()
        for i in range(2):
            if place == 1:
                outs[3 * i + place][...] = dot(hot[i], ref[...], 0, 0).astype(bf16)
            else:
                outs[3 * i + place][...] = dot(ref[...], hot[i]).astype(bf16)


def flipped(row):
    return jnp.broadcast_to(row, (128, row.shape[1])).T[:, :1]


def prepare_kernel(place_ref, own_ref, in_ref, gain_ref, shift_ref, bias_ref, cols_ref, gain_cols, shift_cols):
    size = own_ref.shape[0]
    for ref, half in ((own_ref, place_ref[0]), (in_ref, 1 - place_ref[0])):
        cols_ref[pl.ds(pl.multiple_of(half * size, size), size), :] = ref[...]
    weight = cols_ref[...].astype(f32)
    gain_cols[...] = jnp.sum(weight * gain_ref[...], axis=1, keepdims=True)
    shift_cols[...] = jnp.sum(weight * shift_ref[...], axis=1, keepdims=True) + flipped(bias_ref[1:2, :])


def forward_kernel(*refs):
    place_ref, f_own, f_in, r_mine, r_in, gain_ref, shift_ref, w_ref, bias_ref, gain_cols, shift_cols, *refs = refs
    scaled_ref, turned_ref, pred_ref, base_ref, known_ref, feat_ref = refs
    size = feat_ref.shape[0] // CHIPS
    for ref, y in ((f_own, place_ref[1]), (f_in, 1 - place_ref[1])):
        for i in range(X):
            at = pl.ds(pl.multiple_of(((place_ref[2] ^ i) * YH + y) * size, size), size)
            feat_ref[at, :] = ref[i * size : (i + 1) * size, :]
    feats = feat_ref[...].astype(f32)
    row_mean = jnp.mean(feats, axis=0, keepdims=True)
    variance = jnp.mean(feats * feats, axis=0, keepdims=True) - row_mean * row_mean
    inv_std = lax.rsqrt(variance + epsilon)
    normed = (feats - row_mean) * inv_std
    scaled_ref[...] = (normed * flipped(gain_ref[...]) + flipped(shift_ref[...])).astype(bf16)
    rows = scaled_ref.shape[1]
    turned_ref[...] = jnp.concatenate([scaled_ref[...], jnp.zeros((scaled_ref.shape[0], -rows % 128), bf16)], 1).T[:rows]
    predicted = dot(w_ref[...], scaled_ref[...]) + flipped(bias_ref[1:2, :])
    pred_ref[...] = predicted
    known_ref[0:1, :] = row_mean
    known_ref[1:2, :] = inv_std
    known_ref[2:4, :] = jnp.zeros((2, row_mean.shape[1]), f32)
    for i, with_this in enumerate((predicted, gain_cols[...], shift_cols[...])):
        known_ref[4 + i : 5 + i, :] = jnp.sum(predicted * with_this, axis=0, keepdims=True)
    known_ref[7:8, :] = jnp.zeros((1, row_mean.shape[1]), f32)
    own = r_mine.shape[0]
    for ref, half in ((r_mine, place_ref[0]), (r_in, 1 - place_ref[0])):
        base_ref[pl.ds(pl.multiple_of(half * own, own), own), :] = ref[...].astype(f32)
    base_ref[...] = base_ref[...] + flipped(bias_ref[0:1, :])


def target_kernel(*refs):
    blocks, refs = refs[: X + 1], refs[X + 1 :]
    base_ref, pred_ref, gain_ref, shift_ref, known_ref, target_ref, sums_ref, block_ref, sems = refs
    copies = [pltpu.make_async_copy(b, block_ref.at[i], sems.at[i]) for i, b in enumerate(blocks[1:])]
    for copy in copies:
        copy.start()
    total = blocks[0][...]
    for i, copy in enumerate(copies):
        copy.wait()
        total = total + block_ref[i].astype(f32)
    rows = total.shape[0]
    total = jnp.concatenate([total, jnp.zeros((-rows % 128, total.shape[1]), f32)], 0)
    target = total.T[:, :rows] + base_ref[...]
    target_ref[...] = target
    predicted = pred_ref[...]
    sums = [
        jnp.sum(target * with_this, axis=0, keepdims=True)
        for with_this in (predicted, target, gain_ref[...], shift_ref[...])
    ]
    sums = jnp.concatenate(sums + [known_ref[4:8, :]], 0)
    for chip in range(CHIPS):
        sums_ref[chip] = sums


def grad_kernel(place_ref, sums_ref, target_ref, pred_ref, pg_ref, mine_ref, send_ref, rows_ref):
    totals = jnp.sum(sums_ref[...], axis=0)
    cross_sum, targ_sq, targ_gain, targ_shift, pred_sq, pred_gain, pred_shift = [
        totals[i : i + 1, :] for i in range(7)
    ]
    pred_inv = lax.rsqrt(pred_sq + epsilon)
    targ_inv = lax.rsqrt(targ_sq + epsilon)
    cosine = cross_sum * pred_inv * targ_inv
    a_row = pred_inv * targ_inv
    b_row = cosine * pred_inv * pred_inv
    own, rows = mine_ref.shape
    pg_ref[:, :rows] = (-LOSS_SCALE * (target_ref[...] * a_row - b_row * pred_ref[...])).astype(bf16)
    pg_ref[:, rows:] = jnp.zeros((pg_ref.shape[0], pg_ref.shape[1] - rows), bf16)
    mine_ref[...] = pg_ref[pl.ds(pl.multiple_of(place_ref[0] * own, own), own), :rows]
    send_ref[...] = pg_ref[pl.ds(pl.multiple_of((1 - place_ref[0]) * own, own), own), :rows]
    rows_ref[0:1, :] = -LOSS_SCALE * (a_row * targ_gain - b_row * pred_gain)
    rows_ref[1:2, :] = -LOSS_SCALE * (
        cosine * epsilon * pred_inv * pred_inv - (a_row * targ_shift - b_row * pred_shift)
    )
    rows_ref[2:3, :] = 1.0 - cosine
    rows_ref[3:8, :] = jnp.zeros((5, totals.shape[1]), f32)


def on_device(
    teacher_hidden,
    teacher_down,
    teacher_bias,
    teacher_resid,
    student_feat,
    norm_gain,
    norm_shift,
    head_weight,
    head_bias,
    mask_index,
):
    masked = mask_index.shape[1]
    half = masked // 2
    patches, depth = teacher_hidden.shape
    feat_own = student_feat.shape[1]
    full_width, cols_own = head_weight.shape
    feat_chip, cols = 2 * feat_own, 2 * cols_own
    t = lax.axis_index("tensor")
    b = lax.axis_index("batch")
    core, yh, x = t & 1, (t >> 1) & 1, t >> 2
    yl, z = b // Z, b % Z
    place = jnp.stack([core, yh, x]).astype(jnp.int32)

    def in_order(bit, mine, other, axis=0):
        return jnp.where(
            bit == 0,
            jnp.concatenate([mine, other], axis),
            jnp.concatenate([other, mine], axis),
        )

    def rows_at(a, index, size):
        return lax.dynamic_slice_in_dim(a, index * size, size, 0)

    def four_in_order(index, blocks):
        low = [jnp.where(index & 1 == 0, blocks[i], blocks[i ^ 1]) for i in range(4)]
        return [jnp.where(index & 2 == 0, low[i], low[i ^ 2]) for i in range(4)]

    w_own = head_weight.T
    w_in = to_core(w_own)
    kinds = [shape(n, bf16) for n in ((feat_own, half), (half, depth), (cols_own, half))]
    f_other, h_other, r_other, f_mine, h_mine, r_mine = call(
        gather_kernel,
        [*kinds, *kinds],
        [SMEM] + [HBM] * 4,
        [
            pltpu.VMEM(mask_index.shape, jnp.int32),
            pltpu.VMEM((feat_own, patches), bf16),
            pltpu.VMEM((patches, depth), bf16),
            pltpu.VMEM((cols_own, patches), bf16),
            pltpu.SemaphoreType.DMA((4,)),
        ],
        limit=62,
        flops=2 * masked * patches * (feat_own + cols_own + depth),
        moved=2 * patches * (feat_own + cols_own + depth),
        out_spec=ANY,
    )(core[None], mask_index, student_feat.T, teacher_hidden, teacher_resid.T)
    f_in = to_core(f_other)
    f_chip = in_order(core, f_mine, f_in)

    h_other, w_in = lax.optimization_barrier((h_other, w_in))
    part_in = to_core(dot(h_other, teacher_down).astype(bf16))
    f_own = jnp.concatenate([f_chip] + [to_tensor(f_chip, 4 * k) for k in range(1, X)], 0)
    part_own = dot(h_mine, teacher_down).astype(bf16)
    gain, shift = norm_gain[None], norm_shift[None]
    part_own, part_in, f_own = lax.optimization_barrier((part_own, part_in, f_own))

    def both_parts(flip):
        start = ((t >> 1) ^ flip) * cols
        own, arrived = [lax.dynamic_slice_in_dim(a, start, cols, 1).astype(f32) for a in (part_own, part_in)]
        return own + arrived

    far = [both_parts(k).astype(bf16) for k in (5, 3, 7)]
    arrived = [to_tensor(a, 4 * k) for a, k in zip(far, (2, 1, 3), strict=True)]
    part_own, part_in, f_own, _ = lax.optimization_barrier((part_own, part_in, f_own, far))
    f_from = to_tensor(f_own, 2)
    near = [both_parts(k).astype(bf16) for k in (4, 2, 6)]
    near = [to_tensor(a, 4 * k) for a, k in zip(near, (2, 1, 3), strict=True)]
    across = both_parts(1)
    for a in arrived:
        across = across + a.astype(f32)
    near.append(to_tensor(across.astype(bf16), 2))
    own_block = both_parts(0)
    (f_from, w_own, w_in, r_other, bias_own), _ = lax.optimization_barrier(
        ((f_from, w_own, w_in, r_other, (teacher_bias, head_bias)), arrived)
    )
    bias_own = jnp.stack(bias_own)
    biases = in_order(core, bias_own, to_core(bias_own), 1)
    r_in = to_core(r_other)
    w_cols, gain_cols, shift_cols = call(
        prepare_kernel,
        [shape((cols, full_width), bf16), shape((cols, 1), f32), shape((cols, 1), f32)],
        [SMEM, ANY, ANY, VMEM, VMEM, VMEM],
        limit=24,
        flops=4 * cols * full_width,
        moved=6 * cols * full_width,
    )(place, w_own, w_in, gain, shift, biases)
    scaled, scaled_rows, predicted, base, known = call(
        forward_kernel,
        [
            shape((full_width, half), bf16),
            shape((half, full_width), bf16),
            shape((cols, half), f32),
            shape((cols, half), f32),
            shape((8, half), f32),
        ],
        [SMEM] + [ANY] * 4 + [VMEM] * 2 + [ANY] + [VMEM] * 3,
        [pltpu.VMEM((full_width, half), bf16)],
        limit=24,
        flops=2 * cols * full_width * half,
        moved=8 * cols * full_width,
    )(place, f_own, f_from, r_mine, r_in, gain, shift, w_cols, biases, gain_cols, shift_cols)
    row_mean, inv_std = known[0:1], known[1:2]
    gain_chip = lax.dynamic_slice_in_dim(norm_gain, (t >> 1) * feat_chip, feat_chip, 0)[:, None]
    normed_chip = (f_chip.astype(f32) - row_mean) * inv_std
    normed_chip, gain_chip, known = lax.optimization_barrier((normed_chip, gain_chip, known))

    target, own_sums = call(
        target_kernel,
        [shape((cols, half), f32), shape((CHIPS, 8, half), f32)],
        [ANY] + [HBM] * X + [VMEM] * 5,
        [pltpu.VMEM((X, half, cols), bf16), pltpu.SemaphoreType.DMA((X,))],
        limit=16,
        flops=20 * half * cols,
        moved=24 * half * cols,
    )(own_block, *near, base, predicted, gain_cols, shift_cols, known)
    scaled_rows, _ = lax.optimization_barrier((scaled_rows, own_sums))
    scaled_in = to_core(scaled_rows)
    groups = [list(range(c, 2 * CHIPS, 2)) for c in range(2)]
    all_sums = lax.all_to_all(own_sums, "tensor", 0, 0, axis_index_groups=groups)
    pred_grad, pg_mine, pg_send, rows = call(
        grad_kernel,
        [
            shape((cols, half + -half % 128), bf16),
            shape((cols_own, half), bf16),
            shape((cols_own, half), bf16),
            shape((8, half), f32),
        ],
        [SMEM, VMEM, VMEM, VMEM],
        limit=16,
        flops=6 * half * cols,
        moved=10 * half * cols,
    )(place, all_sums, target, predicted)
    pg_in = to_core(pg_send)
    part_a, part_b = 192, 64
    width = full_width // 2
    weight_part = dot(pg_mine, scaled, 1, 1) + dot(pg_in, scaled_in)
    bias_part = jnp.sum(pg_mine.astype(f32), axis=1) + jnp.sum(pg_in.astype(f32), axis=1)

    def part_of(y_half, z_half):
        return (
            lax.dynamic_slice(weight_part, (0, y_half * width), (part_a, width)),
            lax.dynamic_slice(weight_part, (part_a + z_half * part_b, 0), (part_b, full_width)),
        )

    a_keep, b_keep = part_of(yl, z & 1)
    a_send, b_send = [a.astype(bf16) for a in part_of(1 - yl, 1 - (z & 1))]
    pred_grad, _ = lax.optimization_barrier((pred_grad, (a_send, b_send)))
    d_part = dot(w_cols, pred_grad, 0, 0).astype(bf16)
    z0, zg = z & 1, z >> 1
    a_arrived, b_arrived = to_batch(a_send, YL * Z // 2), to_batch(b_send, 1)
    d_in = [to_tensor(rows_at(d_part, x ^ k, YH * feat_chip), 4 * k) for k in (2, 1, 3)]
    a_sum = a_keep + a_arrived.astype(f32)
    b_sum = b_keep + b_arrived.astype(f32)
    a_half, b_half = part_a // 2, width

    a_out = rows_at(a_sum, 1 - z0, a_half).astype(bf16)
    b_out = lax.dynamic_slice_in_dim(b_sum, (1 - yl) * width, width, 1).astype(bf16)
    a_sum = rows_at(a_sum, z0, a_half) + to_batch(a_out, 1).astype(f32)
    b_sum = lax.dynamic_slice_in_dim(b_sum, yl * width, width, 1) + to_batch(
        b_out, YL * Z // 2
    ).astype(f32)
    a_size, b_size = a_half // 4, part_b // 4

    def block_of(group):
        return jnp.concatenate([rows_at(a_sum, group, a_size), rows_at(b_sum, group, b_size)], 0)

    out_blocks = [block_of(zg ^ k).astype(bf16) for k in (1, 2, 3)]

    d_in, _ = lax.optimization_barrier((d_in, (a_out, b_out)))
    d_pair = rows_at(d_part, x, YH * feat_chip).astype(f32)
    for d in d_in:
        d_pair = d_pair + d.astype(f32)
    d_across = to_tensor(rows_at(d_pair, 1 - yh, feat_chip).astype(bf16), 2)
    d_across, _ = lax.optimization_barrier((d_across, out_blocks))
    dscaled = (rows_at(d_pair, yh, feat_chip) + d_across.astype(f32))[:, :half]
    dnormed = dscaled * gain_chip
    feat_grad = (
        inv_std * (dnormed - rows[0:1] / full_width - normed_chip * (rows[1:2] / full_width))
    ).astype(bf16)
    norm_parts = jnp.stack([jnp.sum(dscaled * normed_chip, axis=1), jnp.sum(dscaled, axis=1)])
    fg_in = to_core(rows_at(feat_grad, 1 - core, feat_own))
    norm_out = lax.dynamic_slice_in_dim(norm_parts, (1 - core) * feat_own, feat_own, 1)
    norm_own = lax.dynamic_slice_in_dim(norm_parts, core * feat_own, feat_own, 1)
    loss_part = jnp.full((1,), jnp.sum(rows[2]))
    small_in = to_core(jnp.concatenate([norm_out.reshape(-1), loss_part]))
    small = jnp.concatenate([norm_own.reshape(-1), loss_part]) + small_in
    small = jnp.concatenate([small, bias_part, jnp.zeros((width - small.shape[0] - cols_own,), f32)])

    def with_small(a, small):
        high = lax.reduce_precision(small, 8, 7)
        middle = lax.reduce_precision(small - high, 8, 7)
        terms = jnp.stack([high, middle, small - high - middle]).astype(bf16)
        return jnp.concatenate([a, terms, jnp.zeros((5, width), bf16)], 0)

    def small_of(a):
        return jnp.sum(a[-8:].astype(f32), axis=0)

    block = block_of(zg)
    for k, out in zip((1, 2, 3), out_blocks, strict=True):
        block = block + to_batch(out, 2 * k).astype(f32)
    block = with_small(block.astype(bf16), small)
    got = [to_batch(block, 2 * k) for k in (1, 2, 3)]
    parts = four_in_order(zg, [small_of(a) for a in [block] + got])
    small = (parts[0] + parts[1]) + (parts[2] + parts[3])
    out_blocks = four_in_order(zg, [block] + got)
    a_all = jnp.concatenate([o[:a_size] for o in out_blocks], 0)
    b_all = jnp.concatenate([o[a_size:-8] for o in out_blocks], 0)
    a_all = with_small(a_all, small)
    a_in = to_batch(a_all, 1)
    b_in = to_batch(b_all, YL * Z // 2)
    small = small_of(a_all) + small_of(a_in)
    a_all = in_order(z0, a_all[:-8], a_in[:-8])
    b_all = in_order(yl, b_all, b_in, 1)
    a_all = with_small(a_all, small)
    a_in = to_batch(a_all, YL * Z // 2)
    b_in = to_batch(b_all, 1)
    small = small_of(a_all) + small_of(a_in)
    a_all = in_order(yl, a_all[:-8], a_in[:-8], 1)
    b_all = in_order(z0, b_all, b_in)
    grad_head_weight = jnp.concatenate([a_all, b_all], 0).astype(f32).T
    hot = [
        (lax.broadcasted_iota(jnp.int32, (half, patches), 1) == mask_index[0, i * half : (i + 1) * half, None]).astype(bf16)
        for i in range(2)
    ]
    fg = in_order(core, rows_at(feat_grad, core, feat_own), fg_in, 1)
    grad_student = dot(fg, jnp.concatenate(hot, 0)).astype(bf16).T
    grad_gain = small[:feat_own]
    grad_shift = small[feat_own : 2 * feat_own]
    loss = small[2 * feat_own] / (masked * YL * Z)
    grad_head_bias = small[2 * feat_own + 1 : 2 * feat_own + 1 + cols_own]
    return (loss, grad_student, grad_head_weight, grad_head_bias, grad_gain, grad_shift)


def solution(mesh):
    return jax.shard_map(
        on_device,
        mesh=mesh,
        in_specs=(
            P("batch", "tensor"),
            P("tensor", None),
            P("tensor"),
            P("batch", "tensor"),
            P("batch", "tensor"),
            P(),
            P(),
            P(None, "tensor"),
            P("tensor"),
            P("batch", None),
        ),
        out_specs=(
            P(),
            P("batch", "tensor"),
            P(None, "tensor"),
            P("tensor"),
            P("tensor"),
            P("tensor"),
        ),
        check_vma=False,
    )
```
